512 devices in a mesh: slot: 64 (over y, z), hid: 8 (over x, core).
Axes of the slice: x: 4, y: 4, z: 16, core: 2. Of those that a mesh axis runs over, the one named last changes fastest.
Arguments:
- inputs: bfloat16 [64, 512, 4096], P('slot', None, 'hid'), may hold values from -6 to 6
- cotangent: bfloat16 [64, 512, 4096], P('slot', None, 'hid'), may hold values from -6 to 6
- w_gate: bfloat16 [64, 768, 4096], P('slot', 'hid'), may hold values from -0.09375 to 0.09375
- w_up: bfloat16 [64, 768, 4096], P('slot', 'hid'), may hold values from -0.09375 to 0.09375
- counts: int32 [64], replicated, may hold values from 1 to 512, 24576 in all
- place_now: int32 [64, 1], replicated, may hold values from 0 to 11
- place_next: int32 [64, 1], replicated, may hold values from 0 to 11
- master: float32 [12, 768, 4096], P(None, 'slot', 'hid'), may hold values from -0.21875 to 0.21875
- moment_one: float32 [12, 768, 4096], P(None, 'slot', 'hid'), may hold values from -0.3125 to 0.3125
- moment_two: float32 [12, 768, 4096], P(None, 'slot', 'hid'), may hold values from 0.0001 to 0.01
Outputs:
- new_master: float32 [12, 768, 4096], P(None, 'slot', 'hid')
- new_one: float32 [12, 768, 4096], P(None, 'slot', 'hid')
- new_two: float32 [12, 768, 4096], P(None, 'slot', 'hid')
- next_down: bfloat16 [64, 768, 4096], P('slot', 'hid')
The draws below stay inside these ranges and needn't reach their ends.
Inputs may be any that keep to these rules, and one draw needn't show every extreme that they name: `counts`: rows of a slot at or past its count are padding; some slot is full. `place_now`: every expert is held by at least one slot. `place_next`: every expert is held by at least one slot.
All inputs are finite; a program needn't handle non-finite values.
Results may differ from the reference program's by a relative error of at most 0.002.
Values may be sent and summed in bfloat16 or wider, within the bound.
A program may use at most 64 MiB of HBM per device.

```python
import math
import jax
import jax.numpy as jnp
import numpy as np
from jax import lax

D = 4096
FF = 768
EXPERTS = 12
CAP = 512
STEP = 100
SLOTS = 64


def block_scale(rng, dims, cuts, least, top_value):
    factor_of = 1.0
    for axis_at, blocks in cuts:
        heights = jax.random.uniform(jax.random.fold_in(jax.random.fold_in(rng, 6), axis_at), (blocks,), jnp.float32, least / len(cuts), top_value / len(cuts))
        factor_of = factor_of * jnp.repeat(jnp.exp(heights), dims[axis_at] // blocks).reshape((-1,) + (1,) * (len(dims) - 1 - axis_at))
    return factor_of


def choose_distinct(own_key, rows, count, top, lift):
    order = jax.random.permutation(jax.random.fold_in(own_key, 1), count)
    pull = order
    for power in range(3):
        pull = pull * pull // count
    pull = pull * lift // count
    tickets = jax.random.randint(jax.random.fold_in(own_key, 2), (rows, count), 0, 4096) + pull
    fixed_rows = jax.random.permutation(jax.random.fold_in(own_key, 3), rows)[jnp.arange(count) % rows]
    tickets = jnp.where(jnp.arange(rows)[:, None] == fixed_rows[None, :], 1 << 14, tickets)
    score = tickets * count + jnp.arange(count)
    return lax.top_k(score.astype(jnp.int32), top)[1].astype(jnp.int32)


def profile(count, total, bound, slope):
    portions = [(1 << 20) // math.isqrt(grade ** slope) + 1 for grade in range(2, count + 1)]
    rest, given = total - bound - (count - 1), [1] * (count - 1)
    while rest > 0:
        free = [i for i in range(count - 1) if given[i] < bound]
        whole, budget = sum([portions[i] for i in free]), rest
        for i in free:
            addition = min(bound - given[i], max(1, budget * portions[i] // whole), rest)
            given[i] = given[i] + addition
            rest = rest - addition
    return np.array([bound] + given)


def uneven_parts(key, count, total, bound, slope):
    if count == 2:
        one = jax.random.randint(key, (), max(1, total - bound), min(bound, total - 1) + 1)
        return jnp.stack([one, total - one])
    lengths = jnp.asarray(profile(count, total, bound, slope), jnp.int32)
    couples = (count - 1) // 2
    source_of, taker = lengths[1:1 + 2 * couples:2], lengths[2:2 + 2 * couples:2]
    slack = jnp.minimum(source_of - 1, bound - taker)
    passed = jax.random.randint(jax.random.fold_in(key, 1), (couples,), 0, 1 << 20) % (slack + 1)
    lengths = lengths.at[1:1 + 2 * couples:2].set(source_of - passed).at[2:2 + 2 * couples:2].set(taker + passed)
    return lengths[jax.random.permutation(jax.random.fold_in(key, 2), count)]


def centred(key, dims, scale, bound, cuts=(), kind=jnp.bfloat16):
    level = block_scale(key, dims, cuts, -0.22, 0.18) if cuts else 1.0
    values = jax.random.normal(key, dims, jnp.float32) * scale * level
    return jnp.minimum(jnp.maximum(values, -bound), bound).astype(kind)


def setup_inputs(seed: int = 0) -> dict:
    keys = jax.random.split(jax.random.key(seed), 11)
    inputs = centred(keys[0], (SLOTS, CAP, D), 1.0, 6.0, ((0, 64), (2, 8)))
    cotangent = centred(keys[1], (SLOTS, CAP, D), 1.0, 6.0, ((0, 64), (2, 8)))
    w_gate = centred(keys[2], (SLOTS, FF, D), D ** -0.5, 0.09375, ((0, 64), (1, 8)))
    w_up = centred(keys[3], (SLOTS, FF, D), D ** -0.5, 0.09375, ((0, 64), (1, 8)))
    counts = uneven_parts(keys[4], SLOTS, SLOTS * CAP * 3 // 4, CAP, 2).astype(jnp.int32)
    place_now = choose_distinct(keys[5], SLOTS, EXPERTS, 1, 1365)
    place_next = choose_distinct(keys[6], SLOTS, EXPERTS, 1, 682)
    master = centred(keys[7], (EXPERTS, FF, D), FF ** -0.5, 0.21875, ((1, 64), (2, 8)), jnp.float32)
    moment_one = centred(keys[8], (EXPERTS, FF, D), 0.02, 0.3125, ((1, 64), (2, 8)), jnp.float32)
    moment_two = jnp.clip(jnp.exp(math.log(0.01) - 4.6051702 * jax.random.uniform(keys[9], (EXPERTS, FF, D), jnp.float32) ** block_scale(keys[9], (EXPERTS, FF, D), ((1, 64), (2, 8)), -0.2, 0.2)), 0.0001, 0.01)
    return {"inputs": inputs, "cotangent": cotangent, "w_gate": w_gate, "w_up": w_up, "counts": counts, "place_now": place_now, "place_next": place_next, "master": master, "moment_one": moment_one, "moment_two": moment_two}


def reference(inputs, cotangent, w_gate, w_up, counts, place_now, place_next, master, moment_one, moment_two):
    experts_now = place_now[:, 0]
    row_ids = jnp.arange(CAP, dtype=jnp.int32)
    highest = lax.Precision.HIGHEST

    def one_slot(total, item):
        rows_in, grads_out, gate_w, up_w, count, expert = item
        gate = jnp.dot(rows_in.astype(jnp.float32), gate_w.astype(jnp.float32).T, precision=highest)
        up = jnp.dot(rows_in.astype(jnp.float32), up_w.astype(jnp.float32).T, precision=highest)
        hidden = (jax.nn.silu(gate) * up).astype(jnp.bfloat16)
        valid = (row_ids < count)[:, None]
        masked = jnp.where(valid, grads_out.astype(jnp.float32), jnp.float32(0.0))
        slot_grad = jnp.dot(hidden.astype(jnp.float32).T, masked, precision=highest)
        index = expert.astype(jnp.int32)
        current = lax.dynamic_index_in_dim(total, index, 0, keepdims=False)
        total = lax.dynamic_update_index_in_dim(total, current + slot_grad, index, 0)
        return (total, None)
    start = jnp.zeros((EXPERTS, FF, D), jnp.float32)
    summed, unused = lax.scan(one_slot, start, (inputs, cotangent, w_gate, w_up, counts, experts_now))
    match = experts_now[None, :] == jnp.arange(EXPERTS, dtype=jnp.int32)[:, None]
    rows = lax.optimization_barrier(jnp.sum(jnp.where(match, counts[None, :], 0), axis=1)).astype(jnp.int32)
    grad = summed / rows.astype(jnp.float32)[:, None, None]
    new_one = 0.9 * moment_one + 0.1 * grad
    new_two = 0.95 * moment_two + 0.05 * grad * grad
    fixed_one = 1.0 - 0.9 ** STEP
    fixed_two = 1.0 - 0.95 ** STEP
    new_master = master - 0.01 * (new_one / fixed_one) / (jnp.sqrt(new_two / fixed_two) + 1e-08)
    next_down = jnp.take(new_master.astype(jnp.bfloat16), place_next[:, 0], axis=0)
    return (new_master, new_one, new_two, next_down)
```

```python
import jax
import jax.numpy as jnp
from jax import lax
from jax.experimental import pallas as pl
from jax.experimental.pallas import tpu as pltpu
from jax.sharding import PartitionSpec as P

STEP = 100
Y, Z, X, CORES = 4, 16, 4, 2
SLOTS, HIDS = Y * Z, X * CORES
EXPERTS = 12
CAP = 512
WIDTH = 512
FEATURES = 4096
UNITS = 96
PIECE = (48, 128)
MESH = pl.DeviceIdType.MESH
F32, BF16 = jnp.float32, jnp.bfloat16


def remote(src, dst, send_sem, recv_sem, target):
    return pltpu.make_async_remote_copy(
        src_ref=src,
        dst_ref=dst,
        send_sem=send_sem,
        recv_sem=recv_sem,
        device_id=target,
        device_id_type=MESH,
    )


def wait_bytes(ref, sem):
    pltpu.make_async_copy(ref, ref, sem).wait()


def low_half(shape):
    return lax.broadcasted_iota(jnp.int32, shape, len(shape) - 2) < 4


def lanes(tile, q):
    return tile[..., 128 * q : 128 * (q + 1)]


def piece_tiles(whole, low, high):
    axis = len(whole.shape) - 2
    tiles = [lanes(whole, q) for q in range(4)]
    first = low_half(tiles[0].shape)
    for q in (0, 2):
        tiles.append(jnp.where(first, lanes(low, q), lanes(high, q + 1)))
    return jnp.concatenate(tiles, axis=axis)


def ring_gather(own, buf, half, sems, slot, hid, work):
    ring_send, ring_recv, mate_send, mate_recv = sems
    x, core = hid // CORES, hid % CORES
    right, left = lax.rem(x + 1, X), lax.rem(x + X - 1, X)
    across = lax.rem(x + 2, X)
    mate = hid + 1 - 2 * core
    ahead = ((slot, right * CORES + core), (slot, left * CORES + core))
    sources = (left, right)

    def part(ref, p):
        return ref.at[pl.ds(p * half, half)]

    started = []

    def start(src, block, p, send_sem, recv_sem, target):
        copy = remote(src, part(buf.at[block], p), send_sem, recv_sem, target)
        copy.start()
        started.append(copy)

    for step in range(2):
        for way in range(2):
            p = step if way == 0 else 1 - step
            start(part(own, p), hid, p, ring_send.at[way, step], ring_recv.at[way, step], ahead[way])
        start(part(own, step), hid, step, mate_send.at[step], mate_recv.at[step], (slot, mate))

    def arrival(step, way):
        chip = sources[way] if step < 2 else across
        p = (step if step < 2 else 0) if way == 0 else (1 - step if step < 2 else 1)
        return chip, p

    def expect(block, p, send_sem, recv_sem):
        ref = part(buf.at[block], p)
        remote(ref, ref, send_sem, recv_sem, (slot, mate)).wait_recv()

    work(hid, None)
    for step in range(3):
        for way in range(2):
            chip, p = arrival(step, way)
            block = chip * CORES + core
            expect(block, p, ring_send.at[way, step], ring_recv.at[way, step])
            ref = part(buf.at[block], p)
            if step == 0:
                start(ref, block, p, ring_send.at[way, 2], ring_recv.at[way, 2], ahead[way])
            at = 2 + 2 * step + way
            start(ref, block, p, mate_send.at[at], mate_recv.at[at], (slot, mate))
        if step == 0:
            for p in range(2):
                expect(mate, p, mate_send.at[p], mate_recv.at[p])
            work(mate, None)
        for way in range(2):
            chip, p = arrival(step, way)
            work(chip * CORES + core, p)
        for way in range(2):
            chip, p = arrival(step, way)
            at = 2 + 2 * step + way
            expect(chip * CORES + 1 - core, p, mate_send.at[at], mate_recv.at[at])
            work(chip * CORES + 1 - core, p)
    return started


def grads_kernel(
    counts_ref, place_ref, x_ref, cot_ref, gate_ref, up_ref, out_ref,
    xs, weights, cot, hidden, send, recv, sel, acc,
    load_sem, x_ring_send, x_ring_recv, x_mate_send, x_mate_recv,
    h_ring_send, h_ring_recv, h_mate_send, h_mate_recv, send_sem, recv_sem,
):
    slot, hid = lax.axis_index("slot"), lax.axis_index("hid")
    x, core = hid // CORES, hid % CORES
    loads = [
        pltpu.make_async_copy(x_ref.at[0], xs.at[hid], load_sem.at[0]),
        pltpu.make_async_copy(gate_ref.at[0], weights.at[pl.ds(0, UNITS)], load_sem.at[1]),
        pltpu.make_async_copy(up_ref.at[0], weights.at[pl.ds(UNITS, UNITS)], load_sem.at[2]),
        pltpu.make_async_copy(cot_ref.at[0], cot, load_sem.at[3]),
    ]
    for load in loads:
        load.start()
    barrier = pltpu.get_barrier_semaphore()
    right, left = lax.rem(x + 1, X), lax.rem(x + X - 1, X)
    for peer in (right * CORES + core, left * CORES + core, hid + 1 - 2 * core):
        pl.semaphore_signal(barrier, inc=1, device_id=(slot, peer), device_id_type=MESH)

    @pl.loop(1, SLOTS)
    def _(d):
        pl.semaphore_signal(barrier, inc=1, device_id=(lax.rem(slot + d, SLOTS), hid), device_id_type=MESH)

    pl.semaphore_wait(barrier, SLOTS - 1 + 3)

    for load in loads:
        load.wait()

    def project(block, p):
        columns = pl.ds(pl.multiple_of(block * WIDTH, WIDTH), WIDTH)
        rows = slice(None) if p is None else slice(p * CAP // 2, (p + 1) * CAP // 2)
        term = lax.dot_general(
            weights[:, columns], xs[block, rows, :], (((1,), (1,)), ((), ())), preferred_element_type=F32
        )
        if p is None:
            first = not begun
            begun.append(block)
            if first:
                acc[...] = term
                return
        acc[:, rows] += term

    begun = []
    started = ring_gather(
        x_ref.at[0], xs, CAP // 2, (x_ring_send, x_ring_recv, x_mate_send, x_mate_recv), slot, hid, project
    )

    expert_of = lax.broadcasted_iota(jnp.int32, (EXPERTS * 16, SLOTS), 0) // 16
    held = jnp.where(place_ref[...] == expert_of, 1.0, 0.0).astype(BF16)
    column = lax.broadcasted_iota(jnp.int32, (SLOTS, SLOTS * 16), 1) // 16
    spread = jnp.where(lax.broadcasted_iota(jnp.int32, column.shape, 0) == column, 1.0, 0.0).astype(BF16)
    wide = jnp.dot(held, spread, preferred_element_type=F32)
    same = (lax.broadcasted_iota(jnp.int32, wide.shape, 0) % 16) == (
        lax.broadcasted_iota(jnp.int32, wide.shape, 1) % 16
    )
    sel[...] = jnp.where(same, wide, 0.0).astype(BF16)

    gate, up = acc[:UNITS], acc[UNITS:]
    value = (gate / (1.0 + jnp.exp(-gate))) * up
    valid = lax.broadcasted_iota(jnp.int32, value.shape, 1) < counts_ref[slot]
    hidden[hid] = jnp.where(valid, value, 0.0).astype(BF16)

    def exchange(block, p):
        size = UNITS if p is None else UNITS // 2
        base = 0 if p is None else p * size
        terms = jnp.dot(hidden[block, base : base + size, :], cot[...], preferred_element_type=F32)
        for pair in range(size // 24):
            top = 24 * pair
            begin, middle, end = (terms[top + 8 * i : top + 8 * (i + 1)] for i in range(3))
            turned = pltpu.roll(middle, 4, 0)
            owner = block * (UNITS // 12) + (base + top) // 12
            send[owner] = piece_tiles(begin, middle, turned).astype(BF16)
            send[owner + 1] = piece_tiles(end, turned, middle).astype(BF16)
        first = block * (UNITS // 12) + base // 12

        @pl.loop(0, size // 12)
        def _(i):
            owner = first + i

            @pl.when(owner != slot)
            def _():
                remote(send.at[owner], recv.at[slot], send_sem, recv_sem, (owner, hid)).start()

    started += ring_gather(
        hidden.at[hid], hidden, UNITS // 2, (h_ring_send, h_ring_recv, h_mate_send, h_mate_recv), slot, hid, exchange
    )
    recv[slot] = send[slot]
    for copy in started:
        copy.wait_send()
    wait_bytes(recv.at[pl.ds(0, SLOTS - 1)], recv_sem)

    tiles = []
    for t in range(3):
        pieces = recv[:, 16 * t : 16 * (t + 1), :].reshape(SLOTS * 16, 128)
        total = jnp.dot(sel[...], pieces, preferred_element_type=F32).reshape(EXPERTS, 16, 128)
        tiles += [total[:, :8], total[:, 8:]]
    odd = slot % 2
    rest = [tiles[4], pltpu.roll(tiles[4], 4, 1), tiles[5], pltpu.roll(tiles[5], 4, 1)]
    for q in range(4):
        columns = slice(128 * q, 128 * (q + 1))

        @pl.when(odd == 0)
        def _():
            out_ref[:, 0:8, columns] = tiles[q]
            out_ref[:, 8:12, columns] = rest[q][:, :4]

        @pl.when(odd == 1)
        def _():
            out_ref[:, 4:12, columns] = tiles[q]
            out_ref[:, 0:4, columns] = rest[q][:, :4]

    wait_bytes(send.at[pl.ds(0, SLOTS - 1)], send_sem)


def summed_grads(counts, place_now, inputs, cotangent, w_gate, w_up):
    anywhere = pl.BlockSpec(memory_space=pltpu.HBM)
    dma = pltpu.SemaphoreType.DMA
    return pl.pallas_call(
        grads_kernel,
        out_shape=jax.ShapeDtypeStruct((EXPERTS, 12, WIDTH), F32),
        in_specs=[
            pl.BlockSpec(memory_space=pltpu.SMEM),
            pl.BlockSpec(memory_space=pltpu.VMEM),
            anywhere, anywhere, anywhere, anywhere,
        ],
        out_specs=pl.BlockSpec(memory_space=pltpu.VMEM),
        scratch_shapes=[
            pltpu.VMEM((HIDS, CAP, WIDTH), BF16),
            pltpu.VMEM((2 * UNITS, FEATURES), BF16),
            pltpu.VMEM((CAP, WIDTH), BF16),
            pltpu.VMEM((HIDS, UNITS, CAP), BF16),
            pltpu.VMEM((SLOTS,) + PIECE, BF16),
            pltpu.VMEM((SLOTS,) + PIECE, BF16),
            pltpu.VMEM((EXPERTS * 16, SLOTS * 16), BF16),
            pltpu.VMEM((2 * UNITS, CAP), F32),
            dma((4,)),
            dma((2, 3)), dma((2, 3)), dma((8,)), dma((8,)),
            dma((2, 3)), dma((2, 3)), dma((8,)), dma((8,)),
            dma, dma,
        ],
        compiler_params=pltpu.CompilerParams(
            collective_id=0, has_side_effects=True, vmem_limit_bytes=40 * 1024 * 1024
        ),
    )(counts, place_now, inputs, cotangent, w_gate, w_up)


def place_kernel(
    place_ref, master_ref, out_ref, buf, stage, land, ring_send, ring_recv, send_sem, recv_sem
):
    slot, hid = lax.axis_index("slot"), lax.axis_index("hid")
    y, z = slot // Z, slot % Z
    x = hid // CORES
    up, down = lax.rem(z + 1, Z), lax.rem(z + Z - 1, Z)
    diagonal = x == y

    barrier = pltpu.get_barrier_semaphore()
    for peer in (up, down):
        pl.semaphore_signal(barrier, inc=1, device_id=(y * Z + peer, hid), device_id_type=MESH)
    for source in range(HIDS):
        @pl.when(jnp.logical_or(jnp.logical_not(diagonal), source != hid))
        def _():
            pl.semaphore_signal(barrier, inc=1, device_id=(x * Z + z, source), device_id_type=MESH)

    @pl.when(diagonal)
    def _():
        pl.semaphore_wait(barrier, HIDS + 1)

    @pl.when(jnp.logical_not(diagonal))
    def _():
        pl.semaphore_wait(barrier, HIDS + 2)

    first, last = master_ref[:, 0:8, :], master_ref[:, 4:12, :]

    @pl.when(slot % 2 == 0)
    def _():
        buf[z] = piece_tiles(first, pltpu.roll(last, 4, 1), last).astype(BF16)

    @pl.when(slot % 2 == 1)
    def _():
        buf[z] = piece_tiles(last, first, pltpu.roll(first, 4, 1)).astype(BF16)

    group = EXPERTS // 2
    ahead = ((y * Z + up, hid), (y * Z + down, hid))
    started = []

    def hop(way, step, g):
        block = lax.rem(z + (Z - step if way == 0 else step), Z)
        ref = buf.at[block, pl.ds(g * group, group)]
        copy = remote(ref, ref, ring_send.at[way, step, g], ring_recv.at[way, step, g], ahead[way])
        copy.start()
        started.append(copy)

    def arrived(way, step, g):
        block = lax.rem(z + (Z - 1 - step if way == 0 else step + 1), Z)
        ref = buf.at[block, pl.ds(g * group, group)]
        remote(ref, ref, ring_send.at[way, step, g], ring_recv.at[way, step, g], ahead[way]).wait_recv()
        return block

    def deliver(block):
        half = block // (Z // 2)
        target = y * CORES + half
        for to in range(Y):
            expert = place_ref[to * Z + z]
            chosen = buf[block, 0]
            for e in range(1, EXPERTS):
                chosen = lax.select(expert == e, buf[block, e], chosen)
            stage[block, to] = chosen
            mine = jnp.logical_and(to == y, target == hid)

            @pl.when(mine)
            def _():
                land[hid, block % (Z // 2)] = chosen

            @pl.when(jnp.logical_not(mine))
            def _():
                remote(
                    stage.at[block, to], land.at[hid, block % (Z // 2)], send_sem, recv_sem, (to * Z + z, target)
                ).start()

    steps = Z // 2
    for g in range(2):
        for way in range(2):
            hop(way, 0, g)
    deliver(z)
    for step in range(steps):
        ready = []
        for g in range(2):
            for way in range(2):
                if step == steps - 1 and g != way:
                    continue
                ready.append(arrived(way, step, g))
                if step < steps - 2 or (step == steps - 2 and g == way):
                    hop(way, step + 1, g)
        deliver(ready[0])
        if step < steps - 1:
            deliver(ready[1])
    for copy in started:
        copy.wait_send()

    @pl.when(diagonal)
    def _():
        wait_bytes(stage.at[pl.ds(0, Z - 2)], send_sem)
        wait_bytes(land.at[pl.ds(0, HIDS - 1)], recv_sem)

    @pl.when(jnp.logical_not(diagonal))
    def _():
        wait_bytes(stage, send_sem)
        wait_bytes(land, recv_sem)

    half = low_half((8, 128))
    for source in range(HIDS):
        columns = []
        for pair in range(Z // 4):
            even, odd = land[source, 2 * pair].astype(F32), land[source, 2 * pair + 1].astype(F32)
            for q in range(4):
                b = slice(32 + 8 * (q // 2), 40 + 8 * (q // 2))
                if q % 2 == 0:
                    middle = jnp.where(half, even[b], pltpu.roll(odd[b], 4, 0))
                else:
                    middle = jnp.where(half, pltpu.roll(even[b], 4, 0), odd[b])
                columns.append((even[8 * q : 8 * q + 8], middle, odd[8 * q : 8 * q + 8]))
        for q in range(4):
            tall = [tile for pair in range(Z // 4) for tile in columns[4 * pair + q]]
            at = WIDTH * source + 128 * q
            out_ref[0, :, at : at + 128] = jnp.concatenate(tall, axis=0).astype(BF16)


def placed(place_next, new_master):
    dma = pltpu.SemaphoreType.DMA
    return pl.pallas_call(
        place_kernel,
        out_shape=jax.ShapeDtypeStruct((1, UNITS, FEATURES), BF16),
        in_specs=[pl.BlockSpec(memory_space=pltpu.SMEM), pl.BlockSpec(memory_space=pltpu.VMEM)],
        out_specs=pl.BlockSpec(memory_space=pltpu.VMEM),
        scratch_shapes=[
            pltpu.VMEM((Z, EXPERTS) + PIECE, BF16),
            pltpu.VMEM((Z, Y) + PIECE, BF16),
            pltpu.VMEM((HIDS, Z // 2) + PIECE, BF16),
            dma((2, Z // 2, 2)), dma((2, Z // 2, 2)), dma, dma,
        ],
        compiler_params=pltpu.CompilerParams(
            collective_id=1, has_side_effects=True, vmem_limit_bytes=40 * 1024 * 1024
        ),
    )(place_next, new_master)


def local(
    inputs, cotangent, w_gate, w_up, counts, place_now, place_next, master, moment_one, moment_two
):
    experts_now = place_now[:, 0]
    summed = summed_grads(counts, experts_now[None, :], inputs, cotangent, w_gate, w_up)
    match = experts_now[None, :] == jnp.arange(EXPERTS, dtype=jnp.int32)[:, None]
    rows = jnp.sum(jnp.where(match, counts[None, :], 0), axis=1)
    grad = summed / rows.astype(F32)[:, None, None]
    new_one = 0.9 * moment_one + 0.1 * grad
    new_two = 0.95 * moment_two + 0.05 * grad * grad
    fixed_one = 1.0 - 0.9**STEP
    fixed_two = 1.0 - 0.95**STEP
    new_master = master - 0.01 * (new_one / fixed_one) / (jnp.sqrt(new_two / fixed_two) + 1e-08)
    next_down = placed(place_next[:, 0], new_master)
    return (new_master, new_one, new_two, next_down)


def solution(mesh):
    sharded = P(None, "slot", "hid")
    return jax.shard_map(
        local,
        mesh=mesh,
        in_specs=(
            P("slot", None, "hid"),
            P("slot", None, "hid"),
            P("slot", "hid", None),
            P("slot", "hid", None),
            P(),
            P(),
            P(),
            sharded,
            sharded,
            sharded,
        ),
        out_specs=(sharded, sharded, sharded, P("slot", "hid", None)),
        check_vma=False,
    )
```

```python
import jax
import jax.numpy as jnp
from jax import lax
from jax.experimental import pallas as pl
from jax.experimental.pallas import tpu as pltpu
from jax.sharding import PartitionSpec as P

STEP = 100
Y, Z, X, CORES = 4, 16, 4, 2
SLOTS, HIDS = Y * Z, X * CORES
EXPERTS = 12
CAP = 512
WIDTH = 512
FEATURES = 4096
UNITS = 96
PIECE = (48, 128)
NEAR = Z // 2 - 2
GROUPS = 3
LAG = 2
MESH = pl.DeviceIdType.MESH
F32, BF16 = jnp.float32, jnp.bfloat16


def adam(grad, master, one, two):
    new_one = 0.9 * one + 0.1 * grad
    new_two = 0.95 * two + 0.05 * grad * grad
    fixed_one, fixed_two = 1.0 - 0.9**STEP, 1.0 - 0.95**STEP
    return (master - 0.01 * (new_one / fixed_one) / (jnp.sqrt(new_two / fixed_two) + 1e-08), new_one, new_two)


def remote(src, dst, send_sem, recv_sem, target):
    return pltpu.make_async_remote_copy(
        src_ref=src,
        dst_ref=dst,
        send_sem=send_sem,
        recv_sem=recv_sem,
        device_id=target,
        device_id_type=MESH,
    )


def wait_bytes(ref, sem):
    pltpu.make_async_copy(ref, ref, sem).wait()


def low_half(shape):
    return lax.broadcasted_iota(jnp.int32, shape, len(shape) - 2) < 4


def lanes(tile, q):
    return tile[..., 128 * q : 128 * (q + 1)]


def piece_tiles(whole, low, high):
    axis = len(whole.shape) - 2
    tiles = [lanes(whole, q) for q in range(4)]
    first = low_half(tiles[0].shape)
    for q in (0, 2):
        tiles.append(jnp.where(first, lanes(low, q), lanes(high, q + 1)))
    return jnp.concatenate(tiles, axis=axis)


def ring_gather(own, buf, half, sems, slot, hid, work):
    ring_send, ring_recv, mate_send, mate_recv = sems
    x, core = hid // CORES, hid % CORES
    right, left = lax.rem(x + 1, X), lax.rem(x + X - 1, X)
    across = lax.rem(x + 2, X)
    mate = hid + 1 - 2 * core
    ahead = ((slot, right * CORES + core), (slot, left * CORES + core))
    sources = (left, right)

    def part(ref, p):
        return ref.at[pl.ds(p * half, half)]

    started = []

    def start(src, block, p, send_sem, recv_sem, target):
        copy = remote(src, part(buf.at[block], p), send_sem, recv_sem, target)
        copy.start()
        started.append(copy)

    for step in range(2):
        for way in range(2):
            p = step if way == 0 else 1 - step
            start(part(own, p), hid, p, ring_send.at[way, step], ring_recv.at[way, step], ahead[way])
        start(part(own, step), hid, step, mate_send.at[step], mate_recv.at[step], (slot, mate))

    def arrival(step, way):
        chip = sources[way] if step < 2 else across
        p = (step if step < 2 else 0) if way == 0 else (1 - step if step < 2 else 1)
        return chip, p

    def expect(block, p, send_sem, recv_sem):
        ref = part(buf.at[block], p)
        remote(ref, ref, send_sem, recv_sem, (slot, mate)).wait_recv()

    work(hid, None)
    for step in range(3):
        for way in range(2):
            chip, p = arrival(step, way)
            block = chip * CORES + core
            expect(block, p, ring_send.at[way, step], ring_recv.at[way, step])
            ref = part(buf.at[block], p)
            if step == 0:
                start(ref, block, p, ring_send.at[way, 2], ring_recv.at[way, 2], ahead[way])
            at = 2 + 2 * step + way
            start(ref, block, p, mate_send.at[at], mate_recv.at[at], (slot, mate))
        if step == 0:
            for p in range(2):
                expect(mate, p, mate_send.at[p], mate_recv.at[p])
            work(mate, None)
        for way in range(2):
            chip, p = arrival(step, way)
            work(chip * CORES + core, p)
        for way in range(2):
            chip, p = arrival(step, way)
            at = 2 + 2 * step + way
            expect(chip * CORES + 1 - core, p, mate_send.at[at], mate_recv.at[at])
            work(chip * CORES + 1 - core, p)
    return started


def step_kernel(
    counts_ref, held_ref, share_ref, next_ref, x_ref, cot_ref, gate_ref, up_ref, master_ref, one_ref, two_ref,
    grad_ref, out_ref,
    xs, weights, cot, hidden, send, recv, sel, rows, acc, grad, master, one, two, buf, stage, picked, far, farthest, column, land,
    load_sem, x_ring_send, x_ring_recv, x_mate_send, x_mate_recv,
    h_ring_send, h_ring_recv, h_mate_send, h_mate_recv, send_sem, recv_sem,
    ring_send, ring_recv, far_send, far_recv, y_send, y_recv, row_send, row_recv,
):
    slot, hid = lax.axis_index("slot"), lax.axis_index("hid")
    y, z = slot // Z, slot % Z
    loads = [
        pltpu.make_async_copy(x_ref.at[0], xs.at[hid], load_sem.at[0]),
        pltpu.make_async_copy(gate_ref.at[0], weights.at[pl.ds(0, UNITS)], load_sem.at[1]),
        pltpu.make_async_copy(up_ref.at[0], weights.at[pl.ds(UNITS, UNITS)], load_sem.at[2]),
        pltpu.make_async_copy(cot_ref.at[0], cot, load_sem.at[3]),
        pltpu.make_async_copy(master_ref, master, load_sem.at[4]),
        pltpu.make_async_copy(one_ref, one, load_sem.at[5]),
        pltpu.make_async_copy(two_ref, two, load_sem.at[6]),
    ]
    for load in loads:
        load.start()
    barrier = pltpu.get_barrier_semaphore()

    @pl.loop(1, HIDS)
    def _(d):
        pl.semaphore_signal(barrier, inc=1, device_id=(slot, lax.rem(hid + d, HIDS)), device_id_type=MESH)

    @pl.loop(1, SLOTS)
    def _(d):
        pl.semaphore_signal(barrier, inc=1, device_id=(lax.rem(slot + d, SLOTS), hid), device_id_type=MESH)

    pl.semaphore_wait(barrier, SLOTS - 1 + HIDS - 1)

    def prepare():
        for load in loads:
            load.wait()
        expert_of = lax.broadcasted_iota(jnp.int32, (EXPERTS * 16, SLOTS), 0) // 16
        match = held_ref[...] == expert_of
        total_rows = jnp.sum(jnp.where(match, share_ref[...].astype(F32), 0.0), axis=1, keepdims=True)
        rows[...] = jnp.broadcast_to(total_rows, rows.shape)
        held = jnp.where(match, 1.0, 0.0).astype(BF16)
        source_of = lax.broadcasted_iota(jnp.int32, (SLOTS, SLOTS * 16), 1) // 16
        spread = jnp.where(lax.broadcasted_iota(jnp.int32, source_of.shape, 0) == source_of, 1.0, 0.0).astype(BF16)
        wide = jnp.dot(held, spread, preferred_element_type=F32)
        same = (lax.broadcasted_iota(jnp.int32, wide.shape, 0) % 16) == (
            lax.broadcasted_iota(jnp.int32, wide.shape, 1) % 16
        )
        sel[...] = jnp.where(same, wide, 0.0).astype(BF16)

    def project(block, p):
        if p is None and not begun:
            prepare()
        columns = pl.ds(pl.multiple_of(block * WIDTH, WIDTH), WIDTH)
        rows = slice(None) if p is None else slice(p * CAP // 2, (p + 1) * CAP // 2)
        term = lax.dot_general(
            weights[:, columns], xs[block, rows, :], (((1,), (1,)), ((), ())), preferred_element_type=F32
        )
        if p is None:
            first = not begun
            begun.append(block)
            if first:
                acc[...] = term
                return
        acc[:, rows] += term

    begun = []
    started = ring_gather(
        x_ref.at[0], xs, CAP // 2, (x_ring_send, x_ring_recv, x_mate_send, x_mate_recv), slot, hid, project
    )

    gate, up = acc[:UNITS], acc[UNITS:]
    value = (gate / (1.0 + jnp.exp(-gate))) * up
    valid = lax.broadcasted_iota(jnp.int32, value.shape, 1) < counts_ref[slot]
    hidden[hid] = jnp.where(valid, value, 0.0).astype(BF16)

    def exchange(block, p):
        size = UNITS if p is None else UNITS // 2
        base = 0 if p is None else p * size
        terms = jnp.dot(hidden[block, base : base + size, :], cot[...], preferred_element_type=F32)
        for pair in range(size // 24):
            top = 24 * pair
            begin, middle, end = (terms[top + 8 * i : top + 8 * (i + 1)] for i in range(3))
            turned = pltpu.roll(middle, 4, 0)
            owner = block * (UNITS // 12) + (base + top) // 12
            send[owner] = piece_tiles(begin, middle, turned).astype(BF16)
            send[owner + 1] = piece_tiles(end, turned, middle).astype(BF16)
        first = block * (UNITS // 12) + base // 12
        count = size // 12

        @pl.loop(0, count)
        def _(i):
            owner = first + lax.rem(z + i, count)
            @pl.when(owner != slot)
            def _():
                remote(send.at[owner], recv.at[slot], send_sem, recv_sem, (owner, hid)).start()

    started += ring_gather(
        hidden.at[hid], hidden, UNITS // 2, (h_ring_send, h_ring_recv, h_mate_send, h_mate_recv), slot, hid, exchange
    )
    recv[slot] = send[slot]
    for copy in started:
        copy.wait_send()
    wait_bytes(recv.at[pl.ds(0, SLOTS - 1)], recv_sem)

    tiles = []
    for t in range(3):
        pieces = recv[:, 16 * t : 16 * (t + 1), :].reshape(SLOTS * 16, 128)
        total = jnp.dot(sel[...], pieces, preferred_element_type=F32) / rows[...]
        total = total.reshape(EXPERTS, 16, 128)
        tiles += [total[:, :8], total[:, 8:]]
    odd = slot % 2
    rest = [tiles[4], pltpu.roll(tiles[4], 4, 1), tiles[5], pltpu.roll(tiles[5], 4, 1)]
    for q in range(4):
        columns = slice(128 * q, 128 * (q + 1))

        @pl.when(odd == 0)
        def _():
            grad[:, 0:8, columns] = tiles[q]
            grad[:, 8:12, columns] = rest[q][:, :4]

        @pl.when(odd == 1)
        def _():
            grad[:, 4:12, columns] = tiles[q]
            grad[:, 0:4, columns] = rest[q][:, :4]

    mean = grad[...]
    grad_ref[...] = mean
    grad[...] = adam(mean, master[...], one[...], two[...])[0]

    up, down = lax.rem(z + 1, Z), lax.rem(z + Z - 1, Z)
    first, last = grad[:, 0:8, :], grad[:, 4:12, :]

    @pl.when(slot % 2 == 0)
    def _():
        buf[z] = piece_tiles(first, pltpu.roll(last, 4, 1), last).astype(BF16)

    @pl.when(slot % 2 == 1)
    def _():
        buf[z] = piece_tiles(last, first, pltpu.roll(first, 4, 1)).astype(BF16)

    group = EXPERTS // GROUPS
    ahead = ((y * Z + up, hid), (y * Z + down, hid))
    hops = []

    def reached(way, step):
        return lax.rem(z + (Z - 1 - step if way == 0 else step + 1), Z)

    def hop(way, step, g):
        block = z if step == 0 else reached(way, step - 1)
        ref = buf.at[block, pl.ds(g * group, group)]
        copy = remote(ref, ref, ring_send.at[way, step, g], ring_recv.at[way, step, g], ahead[way])
        copy.start()
        hops.append(copy)

    def pick(block, to, column_z):
        expert = next_ref[to * Z + column_z]
        chosen = buf[block, 0]
        for e in range(1, EXPERTS):
            chosen = lax.select(expert == e, buf[block, e], chosen)
        return chosen

    def far_copy(way, last):
        if last:
            src, dst = far.at[way, pl.ds(Y, Y // 2)], farthest.at[way]
        else:
            src, dst = picked.at[way], far.at[way]
        return remote(src, dst, far_send.at[way, last], far_recv.at[way, last], ahead[way])

    def to_column(block, source=None):
        for d in range(Y):
            to = lax.rem(y + d, Y)
            if source is None:
                chosen = pick(block, to, z)
                if d == 0:
                    column[y, block] = chosen
                    continue
                stage[d - 1, block] = chosen
                ref = stage.at[d - 1, block]
            else:
                ref = source(to)
                if d == 0:
                    column[y, block] = ref[...]
                    continue
            remote(ref, column.at[y, block], y_send, y_recv.at[d - 1, block], (to * Z + z, hid)).start()

    def to_row(block):
        half = block // (Z // 2)
        for d in range(Y):
            source = lax.rem(y + Y - d, Y)
            if d > 0:
                ref = column.at[source, block]
                remote(ref, ref, y_send, y_recv.at[d - 1, block], (slot, hid)).wait_recv()
            target = source * CORES + half

            @pl.when(target == hid)
            def _():
                land[hid, block % (Z // 2)] = column[source, block]

            @pl.when(target != hid)
            def _():
                remote(
                    column.at[source, block], land.at[hid, block % (Z // 2)], row_send, row_recv, (slot, target)
                ).start()

    for g in range(GROUPS):
        for way in range(2):
            hop(way, 0, g)
    to_column(z)
    behind = [[z]]
    for step in range(Z // 2):
        ready = [reached(way, step) for way in range(2)]
        if step < NEAR:
            for g in range(GROUPS):
                for way in range(2):
                    ref = buf.at[ready[way], pl.ds(g * group, group)]
                    remote(ref, ref, ring_send.at[way, step, g], ring_recv.at[way, step, g], ahead[way]).wait_recv()
                    if step < NEAR - 1:
                        hop(way, step + 1, g)
            if step == NEAR - 1:
                for way in range(2):
                    one_on, two_on = (lax.rem(z + Z + d * (1 - 2 * way), Z) for d in (1, 2))
                    for to in range(Y):
                        picked[way, to] = pick(ready[way], to, one_on)
                    for to in range(Y // 2):
                        picked[way, Y + to] = pick(ready[way], way * (Y // 2) + to, two_on)
                    hops.append(far_copy(way, 0))
                    hops[-1].start()
            for way in range(2):
                to_column(ready[way])
        elif step == NEAR:
            for way in range(2):
                far_copy(way, 0).wait_recv()
                hops.append(far_copy(way, 1))
                hops[-1].start()
            for way in range(2):
                to_column(ready[way], lambda to: far.at[way, to])
        else:
            for way in range(2):
                far_copy(way, 1).wait_recv()
            ready = ready[:1]
            to_column(ready[0], lambda to: farthest.at[to // (Y // 2), to % (Y // 2)])
        behind.append(ready)
        if step >= LAG - 1:
            for block in behind[step + 1 - LAG]:
                to_row(block)
    for blocks in behind[Z // 2 + 1 - LAG :]:
        for block in blocks:
            to_row(block)
    wait_bytes(land.at[pl.ds(0, HIDS - 1)], row_recv)

    half = low_half((8, 128))
    for source in range(HIDS):
        columns = []
        for pair in range(Z // 4):
            even, odd = land[source, 2 * pair].astype(F32), land[source, 2 * pair + 1].astype(F32)
            for q in range(4):
                b = slice(32 + 8 * (q // 2), 40 + 8 * (q // 2))
                if q % 2 == 0:
                    middle = jnp.where(half, even[b], pltpu.roll(odd[b], 4, 0))
                else:
                    middle = jnp.where(half, pltpu.roll(even[b], 4, 0), odd[b])
                columns.append((even[8 * q : 8 * q + 8], middle, odd[8 * q : 8 * q + 8]))
        for q in range(4):
            tall = [tile for pair in range(Z // 4) for tile in columns[4 * pair + q]]
            at = WIDTH * source + 128 * q
            out_ref[0, :, at : at + 128] = jnp.concatenate(tall, axis=0).astype(BF16)
    for copy in hops:
        copy.wait_send()
    wait_bytes(send.at[pl.ds(0, SLOTS - 1)], send_sem)
    wait_bytes(stage, y_send)
    wait_bytes(land.at[pl.ds(0, HIDS - 1)], row_send)


def local(
    inputs, cotangent, w_gate, w_up, counts, place_now, place_next, master, moment_one, moment_two
):
    dma = pltpu.SemaphoreType.DMA
    smem, vmem, hbm = (pl.BlockSpec(memory_space=m) for m in (pltpu.SMEM, pltpu.VMEM, pltpu.HBM))
    state = (EXPERTS, 12, WIDTH)
    update = pl.pallas_call(
        step_kernel,
        out_shape=[jax.ShapeDtypeStruct(state, F32)] + [jax.ShapeDtypeStruct((1, UNITS, FEATURES), BF16)],
        in_specs=[smem, vmem, vmem, smem] + [hbm] * 7,
        out_specs=[vmem] * 2,
        scratch_shapes=[
            pltpu.VMEM((HIDS, CAP, WIDTH), BF16),
            pltpu.VMEM((2 * UNITS, FEATURES), BF16),
            pltpu.VMEM((CAP, WIDTH), BF16),
            pltpu.VMEM((HIDS, UNITS, CAP), BF16),
            pltpu.VMEM((SLOTS,) + PIECE, BF16),
            pltpu.VMEM((SLOTS,) + PIECE, BF16),
            pltpu.VMEM((EXPERTS * 16, SLOTS * 16), BF16),
            pltpu.VMEM((EXPERTS * 16, 128), F32),
            pltpu.VMEM((2 * UNITS, CAP), F32),
            pltpu.VMEM(state, F32), pltpu.VMEM(state, F32), pltpu.VMEM(state, F32), pltpu.VMEM(state, F32),
            pltpu.VMEM((Z, EXPERTS) + PIECE, BF16),
            pltpu.VMEM((Y - 1, Z) + PIECE, BF16),
            pltpu.VMEM((2, Y + Y // 2) + PIECE, BF16),
            pltpu.VMEM((2, Y + Y // 2) + PIECE, BF16),
            pltpu.VMEM((2, Y // 2) + PIECE, BF16),
            pltpu.VMEM((Y, Z) + PIECE, BF16),
            pltpu.VMEM((HIDS, Z // 2) + PIECE, BF16),
            dma((7,)),
            dma((2, 3)), dma((2, 3)), dma((8,)), dma((8,)),
            dma((2, 3)), dma((2, 3)), dma((8,)), dma((8,)),
            dma, dma,
            dma((2, NEAR, GROUPS)), dma((2, NEAR, GROUPS)), dma((2, 2)), dma((2, 2)), dma, dma((Y - 1, Z)), dma, dma,
        ],
        compiler_params=pltpu.CompilerParams(
            collective_id=0, has_side_effects=True, vmem_limit_bytes=60 * 1024 * 1024
        ),
    )
    grad, next_down = update(
        counts, place_now[:, 0][None, :], counts[None, :], place_next[:, 0],
        inputs, cotangent, w_gate, w_up, master, moment_one, moment_two,
    )
    return adam(grad, master, moment_one, moment_two) + (next_down,)


def solution(mesh):
    sharded = P(None, "slot", "hid")
    return jax.shard_map(
        local,
        mesh=mesh,
        in_specs=(
            P("slot", None, "hid"),
            P("slot", None, "hid"),
            P("slot", "hid", None),
            P("slot", "hid", None),
            P(),
            P(),
            P(),
            sharded,
            sharded,
            sharded,
        ),
        out_specs=(sharded, sharded, sharded, P("slot", "hid", None)),
        check_vma=False,
    )
```

```python
import jax
import jax.numpy as jnp
from jax import lax
from jax.experimental import pallas as pl
from jax.experimental.pallas import tpu as pltpu
from jax.sharding import PartitionSpec as P

STEP = 100
Y, Z, X, CORES = 4, 16, 4, 2
SLOTS, HIDS = Y * Z, X * CORES
EXPERTS = 12
CAP = 512
WIDTH = 512
FEATURES = 4096
UNITS = 96
PIECE = (48, 128)
NEAR = Z // 2 - 2
GROUPS = 3
LAG = 2
MEET_AT = (1, 5, 9)
MESH = pl.DeviceIdType.MESH
F32, BF16 = jnp.float32, jnp.bfloat16


def adam(grad, master, one, two):
    new_one = 0.9 * one + 0.1 * grad
    new_two = 0.95 * two + 0.05 * grad * grad
    fixed_one, fixed_two = 1.0 - 0.9**STEP, 1.0 - 0.95**STEP
    return (master - 0.01 * (new_one / fixed_one) / (jnp.sqrt(new_two / fixed_two) + 1e-08), new_one, new_two)


def remote(src, dst, send_sem, recv_sem, target):
    return pltpu.make_async_remote_copy(
        src_ref=src,
        dst_ref=dst,
        send_sem=send_sem,
        recv_sem=recv_sem,
        device_id=target,
        device_id_type=MESH,
    )


def wait_bytes(ref, sem):
    pltpu.make_async_copy(ref, ref, sem).wait()


def low_half(shape):
    return lax.broadcasted_iota(jnp.int32, shape, len(shape) - 2) < 4


def lanes(tile, q):
    return tile[..., 128 * q : 128 * (q + 1)]


def piece_tiles(whole, low, high):
    axis = len(whole.shape) - 2
    tiles = [lanes(whole, q) for q in range(4)]
    first = low_half(tiles[0].shape)
    for q in (0, 2):
        tiles.append(jnp.where(first, lanes(low, q), lanes(high, q + 1)))
    return jnp.concatenate(tiles, axis=axis)


EVENLY = (
    ("land", 0), ("beside", 0), ("near", 0), ("other", 0),
    ("land", 1), ("near", 1), ("other", 1),
    ("land", 2), ("near", 2), ("other", 2),
)
ACROSS_FIRST = (
    ("land", 0), ("beside", 0), ("near", 0), ("land", 1),
    ("land", 2), ("near", 2), ("other", 2),
    ("other", 0), ("near", 1), ("other", 1),
)


def ring_gather(own, buf, half, sems, slot, hid, work, order):
    ring_send, ring_recv, mate_send, mate_recv = sems
    x, core = hid // CORES, hid % CORES
    right, left = lax.rem(x + 1, X), lax.rem(x + X - 1, X)
    across = lax.rem(x + 2, X)
    mate = hid + 1 - 2 * core
    ahead = ((slot, right * CORES + core), (slot, left * CORES + core))
    sources = (left, right)

    def part(ref, p):
        return ref.at[pl.ds(p * half, half)]

    started = []

    def start(src, block, p, send_sem, recv_sem, target):
        copy = remote(src, part(buf.at[block], p), send_sem, recv_sem, target)
        copy.start()
        started.append(copy)

    for step in range(2):
        for way in range(2):
            p = step if way == 0 else 1 - step
            start(part(own, p), hid, p, ring_send.at[way, step], ring_recv.at[way, step], ahead[way])
        start(part(own, step), hid, step, mate_send.at[step], mate_recv.at[step], (slot, mate))

    def arrival(step, way):
        chip = sources[way] if step < 2 else across
        p = (step if step < 2 else 0) if way == 0 else (1 - step if step < 2 else 1)
        return chip, p

    def expect(block, p, send_sem, recv_sem):
        ref = part(buf.at[block], p)
        remote(ref, ref, send_sem, recv_sem, (slot, mate)).wait_recv()

    def land(step):
        for way in range(2):
            chip, p = arrival(step, way)
            block = chip * CORES + core
            expect(block, p, ring_send.at[way, step], ring_recv.at[way, step])
            ref = part(buf.at[block], p)
            if step == 0:
                start(ref, block, p, ring_send.at[way, 2], ring_recv.at[way, 2], ahead[way])
            at = 2 + 2 * step + way
            start(ref, block, p, mate_send.at[at], mate_recv.at[at], (slot, mate))

    def near(step):
        for way in range(2):
            chip, p = arrival(step, way)
            work(chip * CORES + core, p)

    def other(step):
        for way in range(2):
            chip, p = arrival(step, way)
            at = 2 + 2 * step + way
            expect(chip * CORES + 1 - core, p, mate_send.at[at], mate_recv.at[at])
            work(chip * CORES + 1 - core, p)

    def beside(step):
        for p in range(2):
            expect(mate, p, mate_send.at[p], mate_recv.at[p])
        work(mate, None)

    work(hid, None)
    moves = {"land": land, "near": near, "other": other, "beside": beside}
    for move, step in order:
        moves[move](step)
    return started


def step_kernel(
    counts_ref, held_ref, share_ref, next_ref, x_ref, cot_ref, gate_ref, up_ref, master_ref, one_ref, two_ref,
    grad_ref, out_ref,
    xs, weights, cot, hidden, send, recv, sel, rows, acc, grad, master, one, two, buf, stage, picked, far, farthest, column, gathered, land,
    load_sem, x_ring_send, x_ring_recv, x_mate_send, x_mate_recv,
    h_ring_send, h_ring_recv, h_mate_send, h_mate_recv, send_sem, recv_sem,
    ring_send, ring_recv, far_send, far_recv, y_send, y_recv, row_send, row_recv, met,
):
    slot, hid = lax.axis_index("slot"), lax.axis_index("hid")
    y, z = slot // Z, slot % Z
    loads = [
        pltpu.make_async_copy(x_ref.at[0], xs.at[hid], load_sem.at[0]),
        pltpu.make_async_copy(gate_ref.at[0], weights.at[pl.ds(0, UNITS)], load_sem.at[1]),
        pltpu.make_async_copy(up_ref.at[0], weights.at[pl.ds(UNITS, UNITS)], load_sem.at[2]),
        pltpu.make_async_copy(cot_ref.at[0], cot, load_sem.at[3]),
        pltpu.make_async_copy(master_ref, master, load_sem.at[4]),
        pltpu.make_async_copy(one_ref, one, load_sem.at[5]),
        pltpu.make_async_copy(two_ref, two, load_sem.at[6]),
    ]
    for load in loads:
        load.start()
    barrier = pltpu.get_barrier_semaphore()

    x, core = hid // CORES, hid % CORES

    def in_line(step):
        return (y * Z + lax.rem(z + Z + step, Z), hid)

    def in_row(step):
        return (lax.rem(y + Y + step, Y) * Z + z, hid)

    greeted = [(slot, lax.rem(x + step, X) * CORES + core) for step in (1, X - 1)] + [(slot, hid + 1 - 2 * core)]
    rounds = [[in_line(step) for step in (1, 2, 3)], [in_line(step) for step in (4, 8, 12)], [in_row(step) for step in (1, 2, 3)]]
    greeted += [in_line(-step) for step in (1, 2, 3, 4, 8, 12)] + [in_row(-step) for step in (1, 2, 3)]
    for peer in greeted:
        pl.semaphore_signal(barrier, inc=1, device_id=peer, device_id_type=MESH)
    pl.semaphore_wait(barrier, len(greeted))

    def meet(at):
        if at > 0:
            pl.semaphore_wait(met.at[at - 1], len(rounds[at - 1]))
        for peer in rounds[at] if at < len(rounds) else ():
            pl.semaphore_signal(met.at[at], inc=1, device_id=peer, device_id_type=MESH)

    def prepare():
        for load in loads:
            load.wait()
        expert_of = lax.broadcasted_iota(jnp.int32, (EXPERTS * 16, SLOTS), 0) // 16
        match = held_ref[...] == expert_of
        total_rows = jnp.sum(jnp.where(match, share_ref[...].astype(F32), 0.0), axis=1, keepdims=True)
        rows[...] = jnp.broadcast_to(total_rows, rows.shape)
        held = jnp.where(match, 1.0, 0.0).astype(BF16)
        source_of = lax.broadcasted_iota(jnp.int32, (SLOTS, SLOTS * 16), 1) // 16
        spread = jnp.where(lax.broadcasted_iota(jnp.int32, source_of.shape, 0) == source_of, 1.0, 0.0).astype(BF16)
        wide = jnp.dot(held, spread, preferred_element_type=F32)
        same = (lax.broadcasted_iota(jnp.int32, wide.shape, 0) % 16) == (
            lax.broadcasted_iota(jnp.int32, wide.shape, 1) % 16
        )
        sel[...] = jnp.where(same, wide, 0.0).astype(BF16)

    def project(block, p):
        calls.append(block)
        if len(calls) in MEET_AT:
            meet(MEET_AT.index(len(calls)))
        if p is None and not begun:
            prepare()
        columns = pl.ds(pl.multiple_of(block * WIDTH, WIDTH), WIDTH)
        rows = slice(None) if p is None else slice(p * CAP // 2, (p + 1) * CAP // 2)
        term = lax.dot_general(
            weights[:, columns], xs[block, rows, :], (((1,), (1,)), ((), ())), preferred_element_type=F32
        )
        if p is None:
            first = not begun
            begun.append(block)
            if first:
                acc[...] = term
                return
        acc[:, rows] += term

    begun, calls = [], []
    started = ring_gather(
        x_ref.at[0], xs, CAP // 2, (x_ring_send, x_ring_recv, x_mate_send, x_mate_recv), slot, hid, project, EVENLY
    )

    meet(len(rounds))
    gate, up = acc[:UNITS], acc[UNITS:]
    value = (gate / (1.0 + jnp.exp(-gate))) * up
    valid = lax.broadcasted_iota(jnp.int32, value.shape, 1) < counts_ref[slot]
    hidden[hid] = jnp.where(valid, value, 0.0).astype(BF16)

    def exchange(block, p):
        size = UNITS if p is None else UNITS // 2
        base = 0 if p is None else p * size
        terms = jnp.dot(hidden[block, base : base + size, :], cot[...], preferred_element_type=F32)
        for pair in range(size // 24):
            top = 24 * pair
            begin, middle, end = (terms[top + 8 * i : top + 8 * (i + 1)] for i in range(3))
            turned = pltpu.roll(middle, 4, 0)
            owner = block * (UNITS // 12) + (base + top) // 12
            send[owner] = piece_tiles(begin, middle, turned).astype(BF16)
            send[owner + 1] = piece_tiles(end, turned, middle).astype(BF16)
        first = block * (UNITS // 12) + base // 12
        count = size // 12

        @pl.loop(0, count)
        def _(i):
            owner = first + lax.rem(z + i, count)
            @pl.when(owner != slot)
            def _():
                remote(send.at[owner], recv.at[slot], send_sem, recv_sem, (owner, hid)).start()

    started += ring_gather(
        hidden.at[hid], hidden, UNITS // 2, (h_ring_send, h_ring_recv, h_mate_send, h_mate_recv), slot, hid, exchange, ACROSS_FIRST
    )
    recv[slot] = send[slot]
    for copy in started:
        copy.wait_send()
    wait_bytes(recv.at[pl.ds(0, SLOTS - 1)], recv_sem)

    tiles = []
    for t in range(3):
        pieces = recv[:, 16 * t : 16 * (t + 1), :].reshape(SLOTS * 16, 128)
        total = jnp.dot(sel[...], pieces, preferred_element_type=F32) / rows[...]
        total = total.reshape(EXPERTS, 16, 128)
        tiles += [total[:, :8], total[:, 8:]]
    odd = slot % 2
    rest = [tiles[4], pltpu.roll(tiles[4], 4, 1), tiles[5], pltpu.roll(tiles[5], 4, 1)]
    for q in range(4):
        columns = slice(128 * q, 128 * (q + 1))

        @pl.when(odd == 0)
        def _():
            grad[:, 0:8, columns] = tiles[q]
            grad[:, 8:12, columns] = rest[q][:, :4]

        @pl.when(odd == 1)
        def _():
            grad[:, 4:12, columns] = tiles[q]
            grad[:, 0:4, columns] = rest[q][:, :4]

    mean = grad[...]
    grad_ref[...] = mean
    grad[...] = adam(mean, master[...], one[...], two[...])[0]

    up, down = lax.rem(z + 1, Z), lax.rem(z + Z - 1, Z)
    first, last = grad[:, 0:8, :], grad[:, 4:12, :]

    @pl.when(slot % 2 == 0)
    def _():
        buf[z] = piece_tiles(first, pltpu.roll(last, 4, 1), last).astype(BF16)

    @pl.when(slot % 2 == 1)
    def _():
        buf[z] = piece_tiles(last, first, pltpu.roll(first, 4, 1)).astype(BF16)

    group = EXPERTS // GROUPS
    ahead = ((y * Z + up, hid), (y * Z + down, hid))
    hops = []

    def reached(way, step):
        return lax.rem(z + (Z - 1 - step if way == 0 else step + 1), Z)

    def hop(way, step, g):
        block = z if step == 0 else reached(way, step - 1)
        ref = buf.at[block, pl.ds(g * group, group)]
        copy = remote(ref, ref, ring_send.at[way, step, g], ring_recv.at[way, step, g], ahead[way])
        copy.start()
        hops.append(copy)

    def pick(block, to, column_z):
        expert = next_ref[to * Z + column_z]
        chosen = buf[block, 0]
        for e in range(1, EXPERTS):
            chosen = lax.select(expert == e, buf[block, e], chosen)
        return chosen

    def far_copy(way, last):
        if last:
            src, dst = far.at[way, pl.ds(Y, Y // 2)], farthest.at[way]
        else:
            src, dst = picked.at[way], far.at[way]
        return remote(src, dst, far_send.at[way, last], far_recv.at[way, last], ahead[way])

    def to_column(at, blocks, source):
        for d in range(Y):
            to = lax.rem(y + d, Y)
            for way, block in enumerate(blocks):
                chosen = source(way, block, to)
                if d == 0:
                    gathered[y, block] = chosen
                else:
                    stage[d - 1, at, way] = chosen
            if d > 0:
                remote(
                    stage.at[d - 1, at, pl.ds(0, len(blocks))],
                    column.at[d - 1, at, pl.ds(0, len(blocks))],
                    y_send, y_recv.at[d - 1, at], (to * Z + z, hid),
                ).start()

    def to_row(at, blocks):
        for d in range(1, Y):
            ref = column.at[d - 1, at, pl.ds(0, len(blocks))]
            remote(ref, ref, y_send, y_recv.at[d - 1, at], (slot, hid)).wait_recv()
            for way, block in enumerate(blocks):
                gathered[lax.rem(y + Y - d, Y), block] = column[d - 1, at, way]
        if at == Z // 2:
            return
        turn = (at + 1) // 2 * (1 if at % 2 == 0 else -1)
        side = 1 - 2 * lax.rem(z, 2)
        pair = lax.rem(z // 2 + side * turn + Z, Z // 2)
        first, half = pair * 2, pair // (Z // 4)
        for source in range(Y):
            target = source * CORES + half
            place = pl.ds(lax.rem(first, Z // 2), 2)

            @pl.when(target == hid)
            def _():
                land[hid, place] = gathered[source, pl.ds(first, 2)]

            @pl.when(target != hid)
            def _():
                remote(
                    gathered.at[source, pl.ds(first, 2)], land.at[hid, place], row_send, row_recv, (slot, target)
                ).start()

    for g in range(GROUPS):
        for way in range(2):
            hop(way, 0, g)
    here = lambda way, block, to: pick(block, to, z)
    to_column(Z // 2, [z], here)
    behind = [(Z // 2, [z])]
    for step in range(Z // 2):
        ready = [reached(way, step) for way in range(2)]
        if step < NEAR:
            for g in range(GROUPS):
                for way in range(2):
                    ref = buf.at[ready[way], pl.ds(g * group, group)]
                    remote(ref, ref, ring_send.at[way, step, g], ring_recv.at[way, step, g], ahead[way]).wait_recv()
                    if step < NEAR - 1:
                        hop(way, step + 1, g)
            if step == NEAR - 1:
                for way in range(2):
                    one_on, two_on = (lax.rem(z + Z + d * (1 - 2 * way), Z) for d in (1, 2))
                    for to in range(Y):
                        picked[way, to] = pick(ready[way], to, one_on)
                    for to in range(Y // 2):
                        picked[way, Y + to] = pick(ready[way], way * (Y // 2) + to, two_on)
                    hops.append(far_copy(way, 0))
                    hops[-1].start()
            to_column(step, ready, here)
        elif step == NEAR:
            for way in range(2):
                far_copy(way, 0).wait_recv()
                hops.append(far_copy(way, 1))
                hops[-1].start()
            to_column(step, ready, lambda way, block, to: far[way, to])
        else:
            for way in range(2):
                far_copy(way, 1).wait_recv()
            ready = ready[:1]
            to_column(step, ready, lambda way, block, to: farthest[to // (Y // 2), to % (Y // 2)])
        behind.append((step, ready))
        if step >= LAG - 1:
            to_row(*behind[step + 1 - LAG])
    for item in behind[Z // 2 + 1 - LAG :]:
        to_row(*item)
    wait_bytes(land.at[pl.ds(0, HIDS - 1)], row_recv)

    half = low_half((8, 128))
    for source in range(HIDS):
        columns = []
        for pair in range(Z // 4):
            even, odd = land[source, 2 * pair].astype(F32), land[source, 2 * pair + 1].astype(F32)
            for q in range(4):
                b = slice(32 + 8 * (q // 2), 40 + 8 * (q // 2))
                if q % 2 == 0:
                    middle = jnp.where(half, even[b], pltpu.roll(odd[b], 4, 0))
                else:
                    middle = jnp.where(half, pltpu.roll(even[b], 4, 0), odd[b])
                columns.append((even[8 * q : 8 * q + 8], middle, odd[8 * q : 8 * q + 8]))
        for q in range(4):
            tall = [tile for pair in range(Z // 4) for tile in columns[4 * pair + q]]
            at = WIDTH * source + 128 * q
            out_ref[0, :, at : at + 128] = jnp.concatenate(tall, axis=0).astype(BF16)
    for copy in hops:
        copy.wait_send()
    wait_bytes(send.at[pl.ds(0, SLOTS - 1)], send_sem)
    wait_bytes(gathered.at[pl.ds(0, Y - 1)], y_send)
    wait_bytes(land.at[pl.ds(0, HIDS - 1)], row_send)


def local(
    inputs, cotangent, w_gate, w_up, counts, place_now, place_next, master, moment_one, moment_two
):
    dma = pltpu.SemaphoreType.DMA
    smem, vmem, hbm = (pl.BlockSpec(memory_space=m) for m in (pltpu.SMEM, pltpu.VMEM, pltpu.HBM))
    state = (EXPERTS, 12, WIDTH)
    update = pl.pallas_call(
        step_kernel,
        out_shape=[jax.ShapeDtypeStruct(state, F32)] + [jax.ShapeDtypeStruct((1, UNITS, FEATURES), BF16)],
        in_specs=[smem, vmem, vmem, smem] + [hbm] * 7,
        out_specs=[vmem] * 2,
        scratch_shapes=[
            pltpu.VMEM((HIDS, CAP, WIDTH), BF16),
            pltpu.VMEM((2 * UNITS, FEATURES), BF16),
            pltpu.VMEM((CAP, WIDTH), BF16),
            pltpu.VMEM((HIDS, UNITS, CAP), BF16),
            pltpu.VMEM((SLOTS,) + PIECE, BF16),
            pltpu.VMEM((SLOTS,) + PIECE, BF16),
            pltpu.VMEM((EXPERTS * 16, SLOTS * 16), BF16),
            pltpu.VMEM((EXPERTS * 16, 128), F32),
            pltpu.VMEM((2 * UNITS, CAP), F32),
            pltpu.VMEM(state, F32), pltpu.VMEM(state, F32), pltpu.VMEM(state, F32), pltpu.VMEM(state, F32),
            pltpu.VMEM((Z, EXPERTS) + PIECE, BF16),
            pltpu.VMEM((Y - 1, Z // 2 + 1, 2) + PIECE, BF16),
            pltpu.VMEM((2, Y + Y // 2) + PIECE, BF16),
            pltpu.VMEM((2, Y + Y // 2) + PIECE, BF16),
            pltpu.VMEM((2, Y // 2) + PIECE, BF16),
            pltpu.VMEM((Y - 1, Z // 2 + 1, 2) + PIECE, BF16),
            pltpu.VMEM((Y, Z) + PIECE, BF16),
            pltpu.VMEM((HIDS, Z // 2) + PIECE, BF16),
            dma((7,)),
            dma((2, 3)), dma((2, 3)), dma((8,)), dma((8,)),
            dma((2, 3)), dma((2, 3)), dma((8,)), dma((8,)),
            dma, dma,
            dma((2, NEAR, GROUPS)), dma((2, NEAR, GROUPS)), dma((2, 2)), dma((2, 2)), dma, dma((Y - 1, Z // 2 + 1)), dma, dma,
            pltpu.SemaphoreType.REGULAR((3,)),
        ],
        compiler_params=pltpu.CompilerParams(
            collective_id=0, has_side_effects=True, vmem_limit_bytes=60 * 1024 * 1024
        ),
    )
    grad, next_down = update(
        counts, place_now[:, 0][None, :], counts[None, :], place_next[:, 0],
        inputs, cotangent, w_gate, w_up, master, moment_one, moment_two,
    )
    return adam(grad, master, moment_one, moment_two) + (next_down,)


def solution(mesh):
    sharded = P(None, "slot", "hid")
    return jax.shard_map(
        local,
        mesh=mesh,
        in_specs=(
            P("slot", None, "hid"),
            P("slot", None, "hid"),
            P("slot", "hid", None),
            P("slot", "hid", None),
            P(),
            P(),
            P(),
            sharded,
            sharded,
            sharded,
        ),
        out_specs=(sharded, sharded, sharded, P("slot", "hid", None)),
        check_vma=False,
    )
```

```python
import jax
import jax.numpy as jnp
from jax import lax
from jax.experimental import pallas as pl
from jax.experimental.pallas import tpu as pltpu
from jax.sharding import PartitionSpec as P

STEP = 100
Y, Z, X, CORES = 4, 16, 4, 2
SLOTS, HIDS = Y * Z, X * CORES
EXPERTS = 12
CAP = 512
WIDTH = 512
FEATURES = 4096
UNITS = 96
PIECE = (48, 128)
NEAR = Z // 2 - 2
GROUPS = 4
LAG = 2
MEET_AT = (1, 5, 9)
MESH = pl.DeviceIdType.MESH
F32, BF16 = jnp.float32, jnp.bfloat16


def adam(grad, master, one, two):
    new_one = 0.9 * one + 0.1 * grad
    new_two = 0.95 * two + 0.05 * grad * grad
    fixed_one, fixed_two = 1.0 - 0.9**STEP, 1.0 - 0.95**STEP
    return (master - 0.01 * (new_one / fixed_one) / (jnp.sqrt(new_two / fixed_two) + 1e-08), new_one, new_two)


def remote(src, dst, send_sem, recv_sem, target):
    return pltpu.make_async_remote_copy(
        src_ref=src,
        dst_ref=dst,
        send_sem=send_sem,
        recv_sem=recv_sem,
        device_id=target,
        device_id_type=MESH,
    )


def wait_bytes(ref, sem):
    pltpu.make_async_copy(ref, ref, sem).wait()


def low_half(shape):
    return lax.broadcasted_iota(jnp.int32, shape, len(shape) - 2) < 4


def lanes(tile, q):
    return tile[..., 128 * q : 128 * (q + 1)]


def piece_tiles(whole, low, high):
    axis = len(whole.shape) - 2
    tiles = [lanes(whole, q) for q in range(4)]
    first = low_half(tiles[0].shape)
    for q in (0, 2):
        tiles.append(jnp.where(first, lanes(low, q), lanes(high, q + 1)))
    return jnp.concatenate(tiles, axis=axis)


EVENLY = (
    ("land", 0), ("beside", 0), ("near", 0), ("other", 0),
    ("land", 1), ("near", 1), ("other", 1),
    ("land", 2), ("near", 2), ("other", 2),
)
ACROSS_FIRST = (
    ("land", 0), ("beside", 0), ("near", 0), ("land", 1),
    ("land", 2), ("near", 2), ("other", 2),
    ("other", 0), ("near", 1), ("other", 1),
)


def ring_gather(own, buf, half, sems, slot, hid, work, order):
    ring_send, ring_recv, mate_send, mate_recv = sems
    x, core = hid // CORES, hid % CORES
    right, left = lax.rem(x + 1, X), lax.rem(x + X - 1, X)
    across = lax.rem(x + 2, X)
    mate = hid + 1 - 2 * core
    ahead = ((slot, right * CORES + core), (slot, left * CORES + core))
    sources = (left, right)

    def part(ref, p):
        return ref.at[pl.ds(p * half, half)]

    started = []

    def start(src, block, p, send_sem, recv_sem, target):
        copy = remote(src, part(buf.at[block], p), send_sem, recv_sem, target)
        copy.start()
        started.append(copy)

    for step in range(2):
        for way in range(2):
            p = step if way == 0 else 1 - step
            start(part(own, p), hid, p, ring_send.at[way, step], ring_recv.at[way, step], ahead[way])
        start(part(own, step), hid, step, mate_send.at[step], mate_recv.at[step], (slot, mate))

    def arrival(step, way):
        chip = sources[way] if step < 2 else across
        p = (step if step < 2 else 0) if way == 0 else (1 - step if step < 2 else 1)
        return chip, p

    def expect(block, p, send_sem, recv_sem):
        ref = part(buf.at[block], p)
        remote(ref, ref, send_sem, recv_sem, (slot, mate)).wait_recv()

    def land(step):
        for way in range(2):
            chip, p = arrival(step, way)
            block = chip * CORES + core
            expect(block, p, ring_send.at[way, step], ring_recv.at[way, step])
            ref = part(buf.at[block], p)
            if step == 0:
                start(ref, block, p, ring_send.at[way, 2], ring_recv.at[way, 2], ahead[way])
            at = 2 + 2 * step + way
            start(ref, block, p, mate_send.at[at], mate_recv.at[at], (slot, mate))

    def near(step):
        for way in range(2):
            chip, p = arrival(step, way)
            work(chip * CORES + core, p)

    def other(step):
        for way in range(2):
            chip, p = arrival(step, way)
            at = 2 + 2 * step + way
            expect(chip * CORES + 1 - core, p, mate_send.at[at], mate_recv.at[at])
            work(chip * CORES + 1 - core, p)

    def beside(step):
        for p in range(2):
            expect(mate, p, mate_send.at[p], mate_recv.at[p])
        work(mate, None)

    work(hid, None)
    moves = {"land": land, "near": near, "other": other, "beside": beside}
    for move, step in order:
        moves[move](step)
    return started


def step_kernel(
    counts_ref, held_ref, share_ref, next_ref, x_ref, cot_ref, gate_ref, up_ref, master_ref, one_ref, two_ref,
    grad_ref, out_ref,
    xs, weights, cot, hidden, send, recv, sel, rows, acc, grad, master, one, two, buf, stage, picked, far, farthest, column, gathered, land,
    load_sem, x_ring_send, x_ring_recv, x_mate_send, x_mate_recv,
    h_ring_send, h_ring_recv, h_mate_send, h_mate_recv, send_sem, recv_sem,
    ring_send, ring_recv, far_send, far_recv, y_send, y_recv, row_send, row_recv, direct_send, direct_recv, met,
):
    slot, hid = lax.axis_index("slot"), lax.axis_index("hid")
    y, z = slot // Z, slot % Z
    loads = [
        pltpu.make_async_copy(x_ref.at[0], xs.at[hid], load_sem.at[0]),
        pltpu.make_async_copy(gate_ref.at[0], weights.at[pl.ds(0, UNITS)], load_sem.at[1]),
        pltpu.make_async_copy(up_ref.at[0], weights.at[pl.ds(UNITS, UNITS)], load_sem.at[2]),
        pltpu.make_async_copy(cot_ref.at[0], cot, load_sem.at[3]),
        pltpu.make_async_copy(master_ref, master, load_sem.at[4]),
        pltpu.make_async_copy(one_ref, one, load_sem.at[5]),
        pltpu.make_async_copy(two_ref, two, load_sem.at[6]),
    ]
    for load in loads:
        load.start()
    barrier = pltpu.get_barrier_semaphore()

    x, core = hid // CORES, hid % CORES

    def in_line(step):
        return (y * Z + lax.rem(z + Z + step, Z), hid)

    def in_row(step):
        return (lax.rem(y + Y + step, Y) * Z + z, hid)

    greeted = [(slot, lax.rem(x + step, X) * CORES + core) for step in (1, X - 1)] + [(slot, hid + 1 - 2 * core)]
    rounds = [[in_line(step) for step in (1, 2, 3)], [in_line(step) for step in (4, 8, 12)], [in_row(step) for step in (1, 2, 3)]]
    greeted += [in_line(-step) for step in (1, 2, 3, 4, 8, 12)] + [in_row(-step) for step in (1, 2, 3)]
    for peer in greeted:
        pl.semaphore_signal(barrier, inc=1, device_id=peer, device_id_type=MESH)
    pl.semaphore_wait(barrier, len(greeted))

    def meet(at):
        if at > 0:
            pl.semaphore_wait(met.at[at - 1], len(rounds[at - 1]))
        for peer in rounds[at] if at < len(rounds) else ():
            pl.semaphore_signal(met.at[at], inc=1, device_id=peer, device_id_type=MESH)

    def prepare():
        for load in loads:
            load.wait()
        expert_of = lax.broadcasted_iota(jnp.int32, (EXPERTS * 16, SLOTS), 0) // 16
        match = held_ref[...] == expert_of
        total_rows = jnp.sum(jnp.where(match, share_ref[...].astype(F32), 0.0), axis=1, keepdims=True)
        rows[...] = jnp.broadcast_to(total_rows, rows.shape)
        held = jnp.where(match, 1.0, 0.0).astype(BF16)
        source_of = lax.broadcasted_iota(jnp.int32, (SLOTS, SLOTS * 16), 1) // 16
        spread = jnp.where(lax.broadcasted_iota(jnp.int32, source_of.shape, 0) == source_of, 1.0, 0.0).astype(BF16)
        wide = jnp.dot(held, spread, preferred_element_type=F32)
        same = (lax.broadcasted_iota(jnp.int32, wide.shape, 0) % 16) == (
            lax.broadcasted_iota(jnp.int32, wide.shape, 1) % 16
        )
        sel[...] = jnp.where(same, wide, 0.0).astype(BF16)

    def project(block, p):
        calls.append(block)
        if len(calls) in MEET_AT:
            meet(MEET_AT.index(len(calls)))
        if p is None and not begun:
            prepare()
        columns = pl.ds(pl.multiple_of(block * WIDTH, WIDTH), WIDTH)
        rows = slice(None) if p is None else slice(p * CAP // 2, (p + 1) * CAP // 2)
        term = lax.dot_general(
            weights[:, columns], xs[block, rows, :], (((1,), (1,)), ((), ())), preferred_element_type=F32
        )
        if p is None:
            first = not begun
            begun.append(block)
            if first:
                acc[...] = term
                return
        acc[:, rows] += term

    begun, calls = [], []
    started = ring_gather(
        x_ref.at[0], xs, CAP // 2, (x_ring_send, x_ring_recv, x_mate_send, x_mate_recv), slot, hid, project, EVENLY
    )

    meet(len(rounds))
    gate, up = acc[:UNITS], acc[UNITS:]
    value = (gate / (1.0 + jnp.exp(-gate))) * up
    valid = lax.broadcasted_iota(jnp.int32, value.shape, 1) < counts_ref[slot]
    hidden[hid] = jnp.where(valid, value, 0.0).astype(BF16)

    def exchange(block, p):
        size = UNITS if p is None else UNITS // 2
        base = 0 if p is None else p * size
        terms = jnp.dot(hidden[block, base : base + size, :], cot[...], preferred_element_type=F32)
        for pair in range(size // 24):
            top = 24 * pair
            begin, middle, end = (terms[top + 8 * i : top + 8 * (i + 1)] for i in range(3))
            turned = pltpu.roll(middle, 4, 0)
            owner = block * (UNITS // 12) + (base + top) // 12
            send[owner] = piece_tiles(begin, middle, turned).astype(BF16)
            send[owner + 1] = piece_tiles(end, turned, middle).astype(BF16)
        first = block * (UNITS // 12) + base // 12
        count = size // 12

        @pl.loop(0, count)
        def _(i):
            owner = first + lax.rem(z + i, count)
            @pl.when(owner != slot)
            def _():
                remote(send.at[owner], recv.at[slot], send_sem, recv_sem, (owner, hid)).start()

    started += ring_gather(
        hidden.at[hid], hidden, UNITS // 2, (h_ring_send, h_ring_recv, h_mate_send, h_mate_recv), slot, hid, exchange, ACROSS_FIRST
    )
    recv[slot] = send[slot]
    for copy in started:
        copy.wait_send()
    wait_bytes(recv.at[pl.ds(0, SLOTS - 1)], recv_sem)

    up, down = lax.rem(z + 1, Z), lax.rem(z + Z - 1, Z)
    group = EXPERTS // GROUPS
    ahead = ((y * Z + up, hid), (y * Z + down, hid))
    hops = []

    def reached(way, step):
        return lax.rem(z + (Z - 1 - step if way == 0 else step + 1), Z)

    def hop(way, step, g):
        block = z if step == 0 else reached(way, step - 1)
        ref = buf.at[block, pl.ds(g * group, group)]
        copy = remote(ref, ref, ring_send.at[way, step, g], ring_recv.at[way, step, g], ahead[way])
        copy.start()
        hops.append(copy)

    def pick(block, to, column_z):
        expert = next_ref[to * Z + column_z]
        chosen = buf[block, 0]
        for e in range(1, EXPERTS):
            chosen = lax.select(expert == e, buf[block, e], chosen)
        return chosen

    def far_copy(way, last):
        if last:
            src, dst = far.at[way, pl.ds(Y, Y // 2)], farthest.at[way]
        else:
            src, dst = picked.at[way], far.at[way]
        return remote(src, dst, far_send.at[way, last], far_recv.at[way, last], ahead[way])

    def to_column(at, blocks, source):
        for d in range(Y):
            to = lax.rem(y + d, Y)
            for way, block in enumerate(blocks):
                chosen = source(way, block, to)
                if d == 0:
                    gathered[y, block] = chosen
                else:
                    stage[d - 1, at, way] = chosen
            if d > 0:
                remote(
                    stage.at[d - 1, at, pl.ds(0, len(blocks))],
                    column.at[d - 1, at, pl.ds(0, len(blocks))],
                    y_send, y_recv.at[d - 1, at], (to * Z + z, hid),
                ).start()

    def to_row(at, blocks):
        for d in range(1, Y):
            ref = column.at[d - 1, at, pl.ds(0, len(blocks))]
            remote(ref, ref, y_send, y_recv.at[d - 1, at], (slot, hid)).wait_recv()
            for way, block in enumerate(blocks):
                gathered[lax.rem(y + Y - d, Y), block] = column[d - 1, at, way]
        if at == Z // 2:
            return
        turn = (at + 1) // 2 * (1 if at % 2 == 0 else -1)
        side = 1 - 2 * lax.rem(z, 2)
        pair = lax.rem(z // 2 + side * turn + Z, Z // 2)
        first = pair * 2
        send_row(first, 2)
        if at == Z // 2 - 2:
            send_row(lax.rem(z - 7 * side + Z, Z), 1)

    def send_row(first, size):
        here, there = pl.ds(first, size), pl.ds(lax.rem(first, Z // 2), size)
        for source in range(Y):
            target = source * CORES + first // (Z // 2)

            @pl.when(target == hid)
            def _():
                land[hid, there] = gathered[source, here]

            @pl.when(target != hid)
            def _():
                remote(gathered.at[source, here], land.at[hid, there], row_send, row_recv, (slot, target)).start()

    def direct(block):
        target = y * CORES + block // (Z // 2)
        for to in range(Y):
            ref = farthest.at[to // (Y // 2), to % (Y // 2)]
            local_one = jnp.logical_and(to == y, target == hid)

            @pl.when(local_one)
            def _():
                land[hid, lax.rem(block, Z // 2)] = ref[...]

            @pl.when(jnp.logical_not(local_one))
            def _():
                remote(
                    ref, land.at[hid, lax.rem(block, Z // 2)], direct_send, direct_recv, (to * Z + z, target)
                ).start()

    def update(part, lines):
        tiles = []
        for t in range(3):
            pieces = recv[:, 16 * t : 16 * (t + 1), :].reshape(SLOTS * 16, 128)
            total = jnp.dot(sel[lines, :], pieces, preferred_element_type=F32) / rows[lines, :]
            total = total.reshape(group, 16, 128)
            tiles += [total[:, :8], total[:, 8:]]
        rest = [tiles[4], pltpu.roll(tiles[4], 4, 1), tiles[5], pltpu.roll(tiles[5], 4, 1)]
        for q in range(4):
            columns = slice(128 * q, 128 * (q + 1))

            @pl.when(slot % 2 == 0)
            def _():
                grad_ref[part, 0:8, columns] = tiles[q]
                grad_ref[part, 8:12, columns] = rest[q][:, :4]

            @pl.when(slot % 2 == 1)
            def _():
                grad_ref[part, 4:12, columns] = tiles[q]
                grad_ref[part, 0:4, columns] = rest[q][:, :4]

        grad[part] = adam(grad_ref[part], master[part], one[part], two[part])[0]
        first, last = grad[part, 0:8, :], grad[part, 4:12, :]

        @pl.when(slot % 2 == 0)
        def _():
            buf[z, part] = piece_tiles(first, pltpu.roll(last, 4, 1), last).astype(BF16)

        @pl.when(slot % 2 == 1)
        def _():
            buf[z, part] = piece_tiles(last, first, pltpu.roll(first, 4, 1)).astype(BF16)

    for g in range(GROUPS):
        update(pl.ds(g * group, group), pl.ds(16 * g * group, 16 * group))
        for way in range(2):
            hop(way, 0, g)
    here = lambda way, block, to: pick(block, to, z)
    to_column(Z // 2, [z], here)
    behind = [(Z // 2, [z])]
    for step in range(Z // 2):
        ready = [reached(way, step) for way in range(2)]
        if step < NEAR:
            for g in range(GROUPS):
                for way in range(2):
                    ref = buf.at[ready[way], pl.ds(g * group, group)]
                    remote(ref, ref, ring_send.at[way, step, g], ring_recv.at[way, step, g], ahead[way]).wait_recv()
                    if step < NEAR - 1:
                        hop(way, step + 1, g)
            if step == NEAR - 1:
                for way in range(2):
                    one_on, two_on = (lax.rem(z + Z + d * (1 - 2 * way), Z) for d in (1, 2))
                    for to in range(Y):
                        picked[way, to] = pick(ready[way], to, one_on)
                    for to in range(Y // 2):
                        picked[way, Y + to] = pick(ready[way], way * (Y // 2) + to, two_on)
                    hops.append(far_copy(way, 0))
                    hops[-1].start()
            to_column(step, ready, here)
        elif step == NEAR:
            for way in range(2):
                far_copy(way, 0).wait_recv()
                hops.append(far_copy(way, 1))
                hops[-1].start()
            to_column(step, ready, lambda way, block, to: far[way, to])
        else:
            for way in range(2):
                far_copy(way, 1).wait_recv()
            direct(ready[0])
        if step < Z // 2 - 1:
            behind.append((step, ready))
        if step >= LAG - 1:
            to_row(*behind[step + 1 - LAG])
    for item in behind[Z // 2 + 1 - LAG :]:
        to_row(*item)
    far_here = lax.rem(z + Z // 2, Z) // (Z // 2) == core
    near_only = jnp.logical_not(far_here)
    diagonal = jnp.logical_and(far_here, x == y)

    @pl.when(near_only)
    def _():
        wait_bytes(land.at[pl.ds(0, HIDS - 1)], row_recv)

    @pl.when(far_here)
    def _():
        wait_bytes(land.at[pl.ds(0, HIDS - 1), pl.ds(0, Z // 2 - 1)], row_recv)

    @pl.when(diagonal)
    def _():
        wait_bytes(recv.at[pl.ds(0, HIDS - 1)], direct_recv)

    @pl.when(jnp.logical_and(far_here, x != y))
    def _():
        wait_bytes(recv.at[pl.ds(0, HIDS)], direct_recv)

    half = low_half((8, 128))
    for source in range(HIDS):
        columns = []
        for pair in range(Z // 4):
            even, odd = land[source, 2 * pair].astype(F32), land[source, 2 * pair + 1].astype(F32)
            for q in range(4):
                b = slice(32 + 8 * (q // 2), 40 + 8 * (q // 2))
                if q % 2 == 0:
                    middle = jnp.where(half, even[b], pltpu.roll(odd[b], 4, 0))
                else:
                    middle = jnp.where(half, pltpu.roll(even[b], 4, 0), odd[b])
                columns.append((even[8 * q : 8 * q + 8], middle, odd[8 * q : 8 * q + 8]))
        for q in range(4):
            tall = [tile for pair in range(Z // 4) for tile in columns[4 * pair + q]]
            at = WIDTH * source + 128 * q
            out_ref[0, :, at : at + 128] = jnp.concatenate(tall, axis=0).astype(BF16)
    for copy in hops:
        copy.wait_send()
    wait_bytes(send.at[pl.ds(0, SLOTS - 1)], send_sem)
    wait_bytes(recv.at[pl.ds(0, (Y - 1) * (Z - 1))], y_send)
    row_pieces = Y * (Z - 1) - Z // 2

    @pl.when(near_only)
    def _():
        wait_bytes(recv.at[pl.ds(0, row_pieces)], row_send)

    @pl.when(far_here)
    def _():
        wait_bytes(recv.at[pl.ds(0, row_pieces + 1)], row_send)

    @pl.when(diagonal)
    def _():
        wait_bytes(recv.at[pl.ds(0, Y - 1)], direct_send)

    @pl.when(jnp.logical_not(diagonal))
    def _():
        wait_bytes(recv.at[pl.ds(0, Y)], direct_send)


def local(
    inputs, cotangent, w_gate, w_up, counts, place_now, place_next, master, moment_one, moment_two
):
    dma = pltpu.SemaphoreType.DMA
    smem, vmem, hbm = (pl.BlockSpec(memory_space=m) for m in (pltpu.SMEM, pltpu.VMEM, pltpu.HBM))
    state = (EXPERTS, 12, WIDTH)
    update = pl.pallas_call(
        step_kernel,
        out_shape=[jax.ShapeDtypeStruct(state, F32)] + [jax.ShapeDtypeStruct((1, UNITS, FEATURES), BF16)],
        in_specs=[smem, vmem, vmem, smem] + [hbm] * 7,
        out_specs=[vmem] * 2,
        scratch_shapes=[
            pltpu.VMEM((HIDS, CAP, WIDTH), BF16),
            pltpu.VMEM((2 * UNITS, FEATURES), BF16),
            pltpu.VMEM((CAP, WIDTH), BF16),
            pltpu.VMEM((HIDS, UNITS, CAP), BF16),
            pltpu.VMEM((SLOTS,) + PIECE, BF16),
            pltpu.VMEM((SLOTS,) + PIECE, BF16),
            pltpu.VMEM((EXPERTS * 16, SLOTS * 16), BF16),
            pltpu.VMEM((EXPERTS * 16, 128), F32),
            pltpu.VMEM((2 * UNITS, CAP), F32),
            pltpu.VMEM(state, F32), pltpu.VMEM(state, F32), pltpu.VMEM(state, F32), pltpu.VMEM(state, F32),
            pltpu.VMEM((Z, EXPERTS) + PIECE, BF16),
            pltpu.VMEM((Y - 1, Z // 2 + 1, 2) + PIECE, BF16),
            pltpu.VMEM((2, Y + Y // 2) + PIECE, BF16),
            pltpu.VMEM((2, Y + Y // 2) + PIECE, BF16),
            pltpu.VMEM((2, Y // 2) + PIECE, BF16),
            pltpu.VMEM((Y - 1, Z // 2 + 1, 2) + PIECE, BF16),
            pltpu.VMEM((Y, Z) + PIECE, BF16),
            pltpu.VMEM((HIDS, Z // 2) + PIECE, BF16),
            dma((7,)),
            dma((2, 3)), dma((2, 3)), dma((8,)), dma((8,)),
            dma((2, 3)), dma((2, 3)), dma((8,)), dma((8,)),
            dma, dma,
            dma((2, NEAR, GROUPS)), dma((2, NEAR, GROUPS)), dma((2, 2)), dma((2, 2)), dma, dma((Y - 1, Z // 2 + 1)), dma, dma, dma, dma,
            pltpu.SemaphoreType.REGULAR((3,)),
        ],
        compiler_params=pltpu.CompilerParams(
            collective_id=0, has_side_effects=True, vmem_limit_bytes=60 * 1024 * 1024
        ),
    )
    grad, next_down = update(
        counts, place_now[:, 0][None, :], counts[None, :], place_next[:, 0],
        inputs, cotangent, w_gate, w_up, master, moment_one, moment_two,
    )
    return adam(grad, master, moment_one, moment_two) + (next_down,)


def solution(mesh):
    sharded = P(None, "slot", "hid")
    return jax.shard_map(
        local,
        mesh=mesh,
        in_specs=(
            P("slot", None, "hid"),
            P("slot", None, "hid"),
            P("slot", "hid", None),
            P("slot", "hid", None),
            P(),
            P(),
            P(),
            sharded,
            sharded,
            sharded,
        ),
        out_specs=(sharded, sharded, sharded, P("slot", "hid", None)),
        check_vma=False,
    )
```

```python
import jax
import jax.numpy as jnp
from jax import lax
from jax.experimental import pallas as pl
from jax.experimental.pallas import tpu as pltpu
from jax.sharding import PartitionSpec as P

STEP = 100
Y, Z, X, CORES = 4, 16, 4, 2
SLOTS, HIDS = Y * Z, X * CORES
EXPERTS = 12
CAP = 512
WIDTH = 512
FEATURES = 4096
UNITS = 96
PIECE = (48, 128)
NEAR = Z // 2 - 2
GROUPS = 4
LAG = 1
MEET_AT = (1, 3, 7)
MESH = pl.DeviceIdType.MESH
F32, BF16 = jnp.float32, jnp.bfloat16


def adam(grad, master, one, two):
    new_one = 0.9 * one + 0.1 * grad
    new_two = 0.95 * two + 0.05 * grad * grad
    fixed_one, fixed_two = 1.0 - 0.9**STEP, 1.0 - 0.95**STEP
    return (master - 0.01 * (new_one / fixed_one) / (jnp.sqrt(new_two / fixed_two) + 1e-08), new_one, new_two)


def remote(src, dst, send_sem, recv_sem, target):
    return pltpu.make_async_remote_copy(
        src_ref=src,
        dst_ref=dst,
        send_sem=send_sem,
        recv_sem=recv_sem,
        device_id=target,
        device_id_type=MESH,
    )


def wait_bytes(ref, sem):
    pltpu.make_async_copy(ref, ref, sem).wait()


def low_half(shape):
    return lax.broadcasted_iota(jnp.int32, shape, len(shape) - 2) < 4


def lanes(tile, q):
    return tile[..., 128 * q : 128 * (q + 1)]


def piece_tiles(whole, low, high):
    axis = len(whole.shape) - 2
    tiles = [lanes(whole, q) for q in range(4)]
    first = low_half(tiles[0].shape)
    for q in (0, 2):
        tiles.append(jnp.where(first, lanes(low, q), lanes(high, q + 1)))
    return jnp.concatenate(tiles, axis=axis)


EVENLY = (
    ("land", 0), ("beside", 0), ("near", 0), ("other", 0),
    ("land", 1), ("near", 1), ("other", 1),
    ("land", 2), ("near", 2), ("other", 2),
)
ACROSS_FIRST = (
    ("land", 0), ("beside", 0), ("near", 0), ("land", 1),
    ("land", 2), ("near", 2), ("other", 2),
    ("other", 0), ("near", 1), ("other", 1),
)


def ring_gather(own, buf, half, sems, slot, hid, work, order):
    ring_send, ring_recv, mate_send, mate_recv = sems
    x, core = hid // CORES, hid % CORES
    right, left = lax.rem(x + 1, X), lax.rem(x + X - 1, X)
    across = lax.rem(x + 2, X)
    mate = hid + 1 - 2 * core
    ahead = ((slot, right * CORES + core), (slot, left * CORES + core))
    sources = (left, right)

    def part(ref, p):
        return ref.at[pl.ds(p * half, half)]

    started = []

    def start(src, block, p, send_sem, recv_sem, target):
        copy = remote(src, part(buf.at[block], p), send_sem, recv_sem, target)
        copy.start()
        started.append(copy)

    for step in range(2):
        for way in range(2):
            p = step if way == 0 else 1 - step
            start(part(own, p), hid, p, ring_send.at[way, step], ring_recv.at[way, step], ahead[way])
        start(part(own, step), hid, step, mate_send.at[step], mate_recv.at[step], (slot, mate))

    def arrival(step, way):
        chip = sources[way] if step < 2 else across
        p = (step if step < 2 else 0) if way == 0 else (1 - step if step < 2 else 1)
        return chip, p

    def expect(block, p, send_sem, recv_sem):
        ref = part(buf.at[block], p)
        remote(ref, ref, send_sem, recv_sem, (slot, mate)).wait_recv()

    def land(step):
        for way in range(2):
            chip, p = arrival(step, way)
            block = chip * CORES + core
            expect(block, p, ring_send.at[way, step], ring_recv.at[way, step])
            ref = part(buf.at[block], p)
            if step == 0:
                start(ref, block, p, ring_send.at[way, 2], ring_recv.at[way, 2], ahead[way])
            at = 2 + 2 * step + way
            start(ref, block, p, mate_send.at[at], mate_recv.at[at], (slot, mate))

    def near(step):
        for way in range(2):
            chip, p = arrival(step, way)
            work(chip * CORES + core, p)

    def other(step):
        for way in range(2):
            chip, p = arrival(step, way)
            at = 2 + 2 * step + way
            expect(chip * CORES + 1 - core, p, mate_send.at[at], mate_recv.at[at])
            work(chip * CORES + 1 - core, p)

    def beside(step):
        for p in range(2):
            expect(mate, p, mate_send.at[p], mate_recv.at[p])
        work(mate, None)

    work(hid, None)
    moves = {"land": land, "near": near, "other": other, "beside": beside}
    for move, step in order:
        moves[move](step)
    return started


def step_kernel(
    counts_ref, held_ref, share_ref, next_ref, x_ref, cot_ref, gate_ref, up_ref, master_ref, one_ref, two_ref,
    mean_ref, out_ref,
    xs, weights, cot, hidden, send, recv, sel, rows, acc, mean, placed, grad, master, one, two, buf, stage, picked, far, farthest, column, gathered, land,
    load_sem, x_ring_send, x_ring_recv, x_mate_send, x_mate_recv,
    h_ring_send, h_ring_recv, h_mate_send, h_mate_recv, send_sem, recv_sem,
    ring_send, ring_recv, far_send, far_recv, y_send, y_recv, row_send, row_recv, direct_send, direct_recv, mean_sem, placed_sem, met,
):
    slot, hid = lax.axis_index("slot"), lax.axis_index("hid")
    y, z = slot // Z, slot % Z
    loads = [
        pltpu.make_async_copy(x_ref.at[0], xs.at[hid], load_sem.at[0]),
        pltpu.make_async_copy(gate_ref.at[0], weights.at[pl.ds(0, UNITS)], load_sem.at[1]),
        pltpu.make_async_copy(up_ref.at[0], weights.at[pl.ds(UNITS, UNITS)], load_sem.at[2]),
        pltpu.make_async_copy(cot_ref.at[0], cot, load_sem.at[3]),
        pltpu.make_async_copy(master_ref, master, load_sem.at[4]),
        pltpu.make_async_copy(one_ref, one, load_sem.at[5]),
        pltpu.make_async_copy(two_ref, two, load_sem.at[6]),
    ]
    for load in loads:
        load.start()
    barrier = pltpu.get_barrier_semaphore()

    x, core = hid // CORES, hid % CORES

    def in_line(step):
        return (y * Z + lax.rem(z + Z + step, Z), hid)

    def in_row(step):
        return (lax.rem(y + Y + step, Y) * Z + z, hid)

    greeted = [(slot, lax.rem(x + step, X) * CORES + core) for step in (1, X - 1)] + [(slot, hid + 1 - 2 * core)]
    rounds = [[in_line(step) for step in (1, 2, 3)], [in_line(step) for step in (4, 8, 12)], [in_row(step) for step in (1, 2, 3)]]
    greeted += [in_line(-step) for step in (1, 2, 3, 4, 8, 12)] + [in_row(-step) for step in (1, 2, 3)]
    for peer in greeted:
        pl.semaphore_signal(barrier, inc=1, device_id=peer, device_id_type=MESH)
    pl.semaphore_wait(barrier, len(greeted))

    def meet(at):
        if at > 0:
            pl.semaphore_wait(met.at[at - 1], len(rounds[at - 1]))
        for peer in rounds[at] if at < len(rounds) else ():
            pl.semaphore_signal(met.at[at], inc=1, device_id=peer, device_id_type=MESH)

    def prepare():
        for load in loads:
            load.wait()
        expert_of = lax.broadcasted_iota(jnp.int32, (EXPERTS * 16, SLOTS), 0) // 16
        match = held_ref[...] == expert_of
        total_rows = jnp.sum(jnp.where(match, share_ref[...].astype(F32), 0.0), axis=1, keepdims=True)
        rows[...] = jnp.broadcast_to(total_rows, rows.shape)
        held = jnp.where(match, 1.0, 0.0).astype(BF16)
        source_of = lax.broadcasted_iota(jnp.int32, (SLOTS, SLOTS * 16), 1) // 16
        spread = jnp.where(lax.broadcasted_iota(jnp.int32, source_of.shape, 0) == source_of, 1.0, 0.0).astype(BF16)
        wide = jnp.dot(held, spread, preferred_element_type=F32)
        same = (lax.broadcasted_iota(jnp.int32, wide.shape, 0) % 16) == (
            lax.broadcasted_iota(jnp.int32, wide.shape, 1) % 16
        )
        sel[...] = jnp.where(same, wide, 0.0).astype(BF16)

    def project(block, p):
        calls.append(block)
        if len(calls) in MEET_AT:
            meet(MEET_AT.index(len(calls)))
        if p is None and not begun:
            prepare()
        columns = pl.ds(pl.multiple_of(block * WIDTH, WIDTH), WIDTH)
        rows = slice(None) if p is None else slice(p * CAP // 2, (p + 1) * CAP // 2)
        term = lax.dot_general(
            weights[:, columns], xs[block, rows, :], (((1,), (1,)), ((), ())), preferred_element_type=F32
        )
        if p is None:
            first = not begun
            begun.append(block)
            if first:
                acc[...] = term
                return
        acc[:, rows] += term

    begun, calls = [], []
    started = ring_gather(
        x_ref.at[0], xs, CAP // 2, (x_ring_send, x_ring_recv, x_mate_send, x_mate_recv), slot, hid, project, EVENLY
    )

    meet(len(rounds))
    gate, up = acc[:UNITS], acc[UNITS:]
    value = (gate / (1.0 + jnp.exp(-gate))) * up
    valid = lax.broadcasted_iota(jnp.int32, value.shape, 1) < counts_ref[slot]
    hidden[hid] = jnp.where(valid, value, 0.0).astype(BF16)

    def exchange(block, p):
        size = UNITS if p is None else UNITS // 2
        base = 0 if p is None else p * size
        terms = jnp.dot(hidden[block, base : base + size, :], cot[...], preferred_element_type=F32)
        for pair in range(size // 24):
            top = 24 * pair
            begin, middle, end = (terms[top + 8 * i : top + 8 * (i + 1)] for i in range(3))
            turned = pltpu.roll(middle, 4, 0)
            owner = block * (UNITS // 12) + (base + top) // 12
            send[owner] = piece_tiles(begin, middle, turned).astype(BF16)
            send[owner + 1] = piece_tiles(end, turned, middle).astype(BF16)
        first = block * (UNITS // 12) + base // 12
        count = size // 12

        @pl.loop(0, count)
        def _(i):
            owner = first + lax.rem(z + i, count)
            @pl.when(owner != slot)
            def _():
                remote(send.at[owner], recv.at[slot], send_sem, recv_sem, (owner, hid)).start()

    started += ring_gather(
        hidden.at[hid], hidden, UNITS // 2, (h_ring_send, h_ring_recv, h_mate_send, h_mate_recv), slot, hid, exchange, ACROSS_FIRST
    )
    recv[slot] = send[slot]
    for copy in started:
        copy.wait_send()
    wait_bytes(recv.at[pl.ds(0, SLOTS - 1)], recv_sem)

    up, down = lax.rem(z + 1, Z), lax.rem(z + Z - 1, Z)
    group = EXPERTS // GROUPS
    ahead = ((y * Z + up, hid), (y * Z + down, hid))
    hops = []

    def reached(way, step):
        return lax.rem(z + (Z - 1 - step if way == 0 else step + 1), Z)

    def hop(way, step, g):
        block = z if step == 0 else reached(way, step - 1)
        ref = buf.at[block, pl.ds(g * group, group)]
        copy = remote(ref, ref, ring_send.at[way, step, g], ring_recv.at[way, step, g], ahead[way])
        copy.start()
        hops.append(copy)

    def pick(block, to, column_z):
        expert = next_ref[to * Z + column_z]
        chosen = buf[block, 0]
        for e in range(1, EXPERTS):
            chosen = lax.select(expert == e, buf[block, e], chosen)
        return chosen

    def far_copy(way, last):
        if last:
            src, dst = far.at[way, pl.ds(Y, Y // 2)], farthest.at[way]
        else:
            src, dst = picked.at[way], far.at[way]
        return remote(src, dst, far_send.at[way, last], far_recv.at[way, last], ahead[way])

    def to_column(at, blocks, source):
        for d in range(Y):
            to = lax.rem(y + d, Y)
            for way, block in enumerate(blocks):
                chosen = source(way, block, to)
                if d == 0:
                    gathered[y, block] = chosen
                else:
                    stage[d - 1, at, way] = chosen
            if d > 0:
                remote(
                    stage.at[d - 1, at, pl.ds(0, len(blocks))],
                    column.at[d - 1, at, pl.ds(0, len(blocks))],
                    y_send, y_recv.at[d - 1, at], (to * Z + z, hid),
                ).start()

    def to_row(at, blocks):
        for d in range(1, Y):
            ref = column.at[d - 1, at, pl.ds(0, len(blocks))]
            remote(ref, ref, y_send, y_recv.at[d - 1, at], (slot, hid)).wait_recv()
            for way, block in enumerate(blocks):
                gathered[lax.rem(y + Y - d, Y), block] = column[d - 1, at, way]
        if at == Z // 2:
            return
        turn = (at + 1) // 2 * (1 if at % 2 == 0 else -1)
        side = 1 - 2 * lax.rem(z, 2)
        pair = lax.rem(z // 2 + side * turn + Z, Z // 2)
        first = pair * 2
        send_row(first, 2)
        if at == Z // 2 - 2:
            send_row(lax.rem(z - 7 * side + Z, Z), 1)

    def send_row(first, size):
        here, there = pl.ds(first, size), pl.ds(lax.rem(first, Z // 2), size)
        for source in range(Y):
            target = source * CORES + first // (Z // 2)

            @pl.when(target == hid)
            def _():
                land[hid, there] = gathered[source, here]

            @pl.when(target != hid)
            def _():
                remote(gathered.at[source, here], land.at[hid, there], row_send, row_recv, (slot, target)).start()

    def direct(block):
        target = y * CORES + block // (Z // 2)
        for to in range(Y):
            ref = farthest.at[to // (Y // 2), to % (Y // 2)]
            local_one = jnp.logical_and(to == y, target == hid)

            @pl.when(local_one)
            def _():
                land[hid, lax.rem(block, Z // 2)] = ref[...]

            @pl.when(jnp.logical_not(local_one))
            def _():
                remote(
                    ref, land.at[hid, lax.rem(block, Z // 2)], direct_send, direct_recv, (to * Z + z, target)
                ).start()

    def update(part, lines):
        tiles = []
        for t in range(3):
            pieces = recv[:, 16 * t : 16 * (t + 1), :].reshape(SLOTS * 16, 128)
            total = jnp.dot(sel[lines, :], pieces, preferred_element_type=F32) / rows[lines, :]
            total = total.reshape(group, 16, 128)
            tiles += [total[:, :8], total[:, 8:]]
        rest = [tiles[4], pltpu.roll(tiles[4], 4, 1), tiles[5], pltpu.roll(tiles[5], 4, 1)]
        for q in range(4):
            columns = slice(128 * q, 128 * (q + 1))

            @pl.when(slot % 2 == 0)
            def _():
                mean[part, 0:8, columns] = tiles[q]
                mean[part, 8:12, columns] = rest[q][:, :4]

            @pl.when(slot % 2 == 1)
            def _():
                mean[part, 4:12, columns] = tiles[q]
                mean[part, 0:4, columns] = rest[q][:, :4]

        grad[part] = adam(mean[part], master[part], one[part], two[part])[0]
        first, last = grad[part, 0:8, :], grad[part, 4:12, :]

        @pl.when(slot % 2 == 0)
        def _():
            buf[z, part] = piece_tiles(first, pltpu.roll(last, 4, 1), last).astype(BF16)

        @pl.when(slot % 2 == 1)
        def _():
            buf[z, part] = piece_tiles(last, first, pltpu.roll(first, 4, 1)).astype(BF16)

    for g in range(GROUPS):
        update(pl.ds(g * group, group), pl.ds(16 * g * group, 16 * group))
        for way in range(2):
            hop(way, 0, g)
    stores = [pltpu.make_async_copy(mean, mean_ref, mean_sem)]
    stores[0].start()
    here = lambda way, block, to: pick(block, to, z)
    to_column(Z // 2, [z], here)
    behind = [(Z // 2, [z])]
    for step in range(Z // 2):
        ready = [reached(way, step) for way in range(2)]
        if step < NEAR:
            for g in range(GROUPS):
                for way in range(2):
                    ref = buf.at[ready[way], pl.ds(g * group, group)]
                    remote(ref, ref, ring_send.at[way, step, g], ring_recv.at[way, step, g], ahead[way]).wait_recv()
                    if step < NEAR - 1:
                        hop(way, step + 1, g)
            if step == NEAR - 1:
                for way in range(2):
                    one_on, two_on = (lax.rem(z + Z + d * (1 - 2 * way), Z) for d in (1, 2))
                    for to in range(Y):
                        picked[way, to] = pick(ready[way], to, one_on)
                    for to in range(Y // 2):
                        picked[way, Y + to] = pick(ready[way], way * (Y // 2) + to, two_on)
                    hops.append(far_copy(way, 0))
                    hops[-1].start()
            to_column(step, ready, here)
        elif step == NEAR:
            for way in range(2):
                far_copy(way, 0).wait_recv()
                hops.append(far_copy(way, 1))
                hops[-1].start()
            to_column(step, ready, lambda way, block, to: far[way, to])
        else:
            for way in range(2):
                far_copy(way, 1).wait_recv()
            direct(ready[0])
        if step < Z // 2 - 1:
            behind.append((step, ready))
        if step >= LAG - 1:
            to_row(*behind[step + 1 - LAG])
    for item in behind[Z // 2 + 1 - LAG :]:
        to_row(*item)
    far_here = lax.rem(z + Z // 2, Z) // (Z // 2) == core
    near_only = jnp.logical_not(far_here)
    diagonal = jnp.logical_and(far_here, x == y)

    @pl.when(near_only)
    def _():
        wait_bytes(land.at[pl.ds(0, HIDS - 1)], row_recv)

    @pl.when(far_here)
    def _():
        wait_bytes(land.at[pl.ds(0, HIDS - 1), pl.ds(0, Z // 2 - 1)], row_recv)

    @pl.when(diagonal)
    def _():
        wait_bytes(recv.at[pl.ds(0, HIDS - 1)], direct_recv)

    @pl.when(jnp.logical_and(far_here, x != y))
    def _():
        wait_bytes(recv.at[pl.ds(0, HIDS)], direct_recv)

    half = low_half((8, 128))
    for source in range(HIDS):
        columns = []
        for pair in range(Z // 4):
            even, odd = land[source, 2 * pair].astype(F32), land[source, 2 * pair + 1].astype(F32)
            for q in range(4):
                b = slice(32 + 8 * (q // 2), 40 + 8 * (q // 2))
                if q % 2 == 0:
                    middle = jnp.where(half, even[b], pltpu.roll(odd[b], 4, 0))
                else:
                    middle = jnp.where(half, pltpu.roll(even[b], 4, 0), odd[b])
                columns.append((even[8 * q : 8 * q + 8], middle, odd[8 * q : 8 * q + 8]))
        for q in range(4):
            tall = [tile for pair in range(Z // 4) for tile in columns[4 * pair + q]]
            at = WIDTH * source + 128 * q
            placed[:, at : at + 128] = jnp.concatenate(tall, axis=0).astype(BF16)
        stores.append(
            pltpu.make_async_copy(
                placed.at[:, pl.ds(WIDTH * source, WIDTH)],
                out_ref.at[0, :, pl.ds(WIDTH * source, WIDTH)],
                placed_sem.at[source],
            )
        )
        stores[-1].start()
    for copy in hops:
        copy.wait_send()
    for copy in stores:
        copy.wait()
    wait_bytes(send.at[pl.ds(0, SLOTS - 1)], send_sem)
    wait_bytes(recv.at[pl.ds(0, (Y - 1) * (Z - 1))], y_send)
    row_pieces = Y * (Z - 1) - Z // 2

    @pl.when(near_only)
    def _():
        wait_bytes(recv.at[pl.ds(0, row_pieces)], row_send)

    @pl.when(far_here)
    def _():
        wait_bytes(recv.at[pl.ds(0, row_pieces + 1)], row_send)

    @pl.when(diagonal)
    def _():
        wait_bytes(recv.at[pl.ds(0, Y - 1)], direct_send)

    @pl.when(jnp.logical_not(diagonal))
    def _():
        wait_bytes(recv.at[pl.ds(0, Y)], direct_send)


def local(
    inputs, cotangent, w_gate, w_up, counts, place_now, place_next, master, moment_one, moment_two
):
    dma = pltpu.SemaphoreType.DMA
    smem, vmem, hbm = (pl.BlockSpec(memory_space=m) for m in (pltpu.SMEM, pltpu.VMEM, pltpu.HBM))
    state = (EXPERTS, 12, WIDTH)
    update = pl.pallas_call(
        step_kernel,
        out_shape=[jax.ShapeDtypeStruct(state, F32)] + [jax.ShapeDtypeStruct((1, UNITS, FEATURES), BF16)],
        in_specs=[smem, vmem, vmem, smem] + [hbm] * 7,
        out_specs=[hbm] * 2,
        scratch_shapes=[
            pltpu.VMEM((HIDS, CAP, WIDTH), BF16),
            pltpu.VMEM((2 * UNITS, FEATURES), BF16),
            pltpu.VMEM((CAP, WIDTH), BF16),
            pltpu.VMEM((HIDS, UNITS, CAP), BF16),
            pltpu.VMEM((SLOTS,) + PIECE, BF16),
            pltpu.VMEM((SLOTS,) + PIECE, BF16),
            pltpu.VMEM((EXPERTS * 16, SLOTS * 16), BF16),
            pltpu.VMEM((EXPERTS * 16, 128), F32),
            pltpu.VMEM((2 * UNITS, CAP), F32),
            pltpu.VMEM(state, F32), pltpu.VMEM((UNITS, FEATURES), BF16),
            pltpu.VMEM(state, F32), pltpu.VMEM(state, F32), pltpu.VMEM(state, F32), pltpu.VMEM(state, F32),
            pltpu.VMEM((Z, EXPERTS) + PIECE, BF16),
            pltpu.VMEM((Y - 1, Z // 2 + 1, 2) + PIECE, BF16),
            pltpu.VMEM((2, Y + Y // 2) + PIECE, BF16),
            pltpu.VMEM((2, Y + Y // 2) + PIECE, BF16),
            pltpu.VMEM((2, Y // 2) + PIECE, BF16),
            pltpu.VMEM((Y - 1, Z // 2 + 1, 2) + PIECE, BF16),
            pltpu.VMEM((Y, Z) + PIECE, BF16),
            pltpu.VMEM((HIDS, Z // 2) + PIECE, BF16),
            dma((7,)),
            dma((2, 3)), dma((2, 3)), dma((8,)), dma((8,)),
            dma((2, 3)), dma((2, 3)), dma((8,)), dma((8,)),
            dma, dma,
            dma((2, NEAR, GROUPS)), dma((2, NEAR, GROUPS)), dma((2, 2)), dma((2, 2)), dma, dma((Y - 1, Z // 2 + 1)), dma, dma, dma, dma, dma, dma((HIDS,)),
            pltpu.SemaphoreType.REGULAR((3,)),
        ],
        compiler_params=pltpu.CompilerParams(
            collective_id=0, has_side_effects=True, vmem_limit_bytes=60 * 1024 * 1024
        ),
    )
    grad, next_down = update(
        counts, place_now[:, 0][None, :], counts[None, :], place_next[:, 0],
        inputs, cotangent, w_gate, w_up, master, moment_one, moment_two,
    )
    return adam(grad, master, moment_one, moment_two) + (next_down,)


def solution(mesh):
    sharded = P(None, "slot", "hid")
    return jax.shard_map(
        local,
        mesh=mesh,
        in_specs=(
            P("slot", None, "hid"),
            P("slot", None, "hid"),
            P("slot", "hid", None),
            P("slot", "hid", None),
            P(),
            P(),
            P(),
            sharded,
            sharded,
            sharded,
        ),
        out_specs=(sharded, sharded, sharded, P("slot", "hid", None)),
        check_vma=False,
    )
```

```python
import jax
import jax.numpy as jnp
from jax import lax
from jax.experimental import pallas as pl
from jax.experimental.pallas import tpu as pltpu
from jax.sharding import PartitionSpec as P

STEP = 100
Y, Z, X, CORES = 4, 16, 4, 2
SLOTS, HIDS = Y * Z, X * CORES
EXPERTS = 12
CAP = 512
WIDTH = 512
FEATURES = 4096
UNITS = 96
PIECE = (48, 128)
NEAR = Z // 2 - 2
GROUPS = 4
LAG = 1
MEET_AT = (1, 3, 7)
MESH = pl.DeviceIdType.MESH
F32, BF16 = jnp.float32, jnp.bfloat16


def adam(grad, master, one, two):
    new_one = 0.9 * one + 0.1 * grad
    new_two = 0.95 * two + 0.05 * grad * grad
    fixed_one, fixed_two = 1.0 - 0.9**STEP, 1.0 - 0.95**STEP
    return (master - 0.01 * (new_one / fixed_one) / (jnp.sqrt(new_two / fixed_two) + 1e-08), new_one, new_two)


def remote(src, dst, send_sem, recv_sem, target):
    return pltpu.make_async_remote_copy(
        src_ref=src,
        dst_ref=dst,
        send_sem=send_sem,
        recv_sem=recv_sem,
        device_id=target,
        device_id_type=MESH,
    )


def wait_bytes(ref, sem):
    pltpu.make_async_copy(ref, ref, sem).wait()


def low_half(shape):
    return lax.broadcasted_iota(jnp.int32, shape, len(shape) - 2) < 4


def lanes(tile, q):
    return tile[..., 128 * q : 128 * (q + 1)]


def piece_tiles(whole, low, high):
    axis = len(whole.shape) - 2
    tiles = [lanes(whole, q) for q in range(4)]
    first = low_half(tiles[0].shape)
    for q in (0, 2):
        tiles.append(jnp.where(first, lanes(low, q), lanes(high, q + 1)))
    return jnp.concatenate(tiles, axis=axis)


EVENLY = (
    ("land", 0), ("beside", 0), ("near", 0), ("other", 0),
    ("land", 1), ("near", 1), ("other", 1),
    ("land", 2), ("near", 2), ("other", 2),
)


def ring_gather(own, buf, half, sems, slot, hid, work, order):
    ring_send, ring_recv, mate_send, mate_recv = sems
    x, core = hid // CORES, hid % CORES
    right, left = lax.rem(x + 1, X), lax.rem(x + X - 1, X)
    across = lax.rem(x + 2, X)
    mate = hid + 1 - 2 * core
    ahead = ((slot, right * CORES + core), (slot, left * CORES + core))
    sources = (left, right)

    def part(ref, p):
        return ref.at[pl.ds(p * half, half)]

    started = []

    def start(src, block, p, send_sem, recv_sem, target):
        copy = remote(src, part(buf.at[block], p), send_sem, recv_sem, target)
        copy.start()
        started.append(copy)

    for step in range(2):
        for way in range(2):
            p = step if way == 0 else 1 - step
            start(part(own, p), hid, p, ring_send.at[way, step], ring_recv.at[way, step], ahead[way])
        start(part(own, step), hid, step, mate_send.at[step], mate_recv.at[step], (slot, mate))

    def arrival(step, way):
        chip = sources[way] if step < 2 else across
        p = (step if step < 2 else 0) if way == 0 else (1 - step if step < 2 else 1)
        return chip, p

    def expect(block, p, send_sem, recv_sem):
        ref = part(buf.at[block], p)
        remote(ref, ref, send_sem, recv_sem, (slot, mate)).wait_recv()

    def land(step):
        for way in range(2):
            chip, p = arrival(step, way)
            block = chip * CORES + core
            expect(block, p, ring_send.at[way, step], ring_recv.at[way, step])
            ref = part(buf.at[block], p)
            if step == 0:
                start(ref, block, p, ring_send.at[way, 2], ring_recv.at[way, 2], ahead[way])
            at = 2 + 2 * step + way
            start(ref, block, p, mate_send.at[at], mate_recv.at[at], (slot, mate))

    def near(step):
        for way in range(2):
            chip, p = arrival(step, way)
            work(chip * CORES + core, p)

    def other(step):
        for way in range(2):
            chip, p = arrival(step, way)
            at = 2 + 2 * step + way
            expect(chip * CORES + 1 - core, p, mate_send.at[at], mate_recv.at[at])
            work(chip * CORES + 1 - core, p)

    def beside(step):
        for p in range(2):
            expect(mate, p, mate_send.at[p], mate_recv.at[p])
        work(mate, None)

    work(hid, None)
    moves = {"land": land, "near": near, "other": other, "beside": beside}
    for move, step in order:
        moves[move](step)
    return started


def step_kernel(
    counts_ref, held_ref, share_ref, next_ref, x_ref, cot_ref, gate_ref, up_ref, master_ref, one_ref, two_ref,
    mean_ref, out_ref,
    xs, weights, cot, hidden, send, recv, sel, rows, acc, mean, placed, grad, master, one, two, buf, stage, picked, far, farthest, column, gathered, land,
    load_sem, x_ring_send, x_ring_recv, x_mate_send, x_mate_recv,
    h_ring_send, h_ring_recv, h_mate_send, h_mate_recv, send_sem, recv_sem,
    ring_send, ring_recv, far_send, far_recv, y_send, y_recv, row_send, row_recv, direct_send, direct_recv, mean_sem, placed_sem, met,
):
    slot, hid = lax.axis_index("slot"), lax.axis_index("hid")
    y, z = slot // Z, slot % Z
    loads = [
        pltpu.make_async_copy(x_ref.at[0], xs.at[hid], load_sem.at[0]),
        pltpu.make_async_copy(gate_ref.at[0], weights.at[pl.ds(0, UNITS)], load_sem.at[1]),
        pltpu.make_async_copy(up_ref.at[0], weights.at[pl.ds(UNITS, UNITS)], load_sem.at[2]),
        pltpu.make_async_copy(cot_ref.at[0], cot, load_sem.at[3]),
        pltpu.make_async_copy(master_ref, master, load_sem.at[4]),
        pltpu.make_async_copy(one_ref, one, load_sem.at[5]),
        pltpu.make_async_copy(two_ref, two, load_sem.at[6]),
    ]
    barrier = pltpu.get_barrier_semaphore()

    x, core = hid // CORES, hid % CORES

    def in_line(step):
        return (y * Z + lax.rem(z + Z + step, Z), hid)

    def in_row(step):
        return (lax.rem(y + Y + step, Y) * Z + z, hid)

    greeted = [(slot, lax.rem(x + step, X) * CORES + core) for step in (1, X - 1)] + [(slot, hid + 1 - 2 * core)]
    rounds = [[in_line(step) for step in (1, 2, 3)], [in_line(step) for step in (4, 8, 12)], [in_row(step) for step in (1, 2, 3)]]
    greeted += [in_line(-step) for step in (1, 2, 3, 4, 8, 12)] + [in_row(-step) for step in (1, 2, 3)]
    for peer in greeted:
        pl.semaphore_signal(barrier, inc=1, device_id=peer, device_id_type=MESH)
    for load in loads:
        load.start()
    pl.semaphore_wait(barrier, len(greeted))

    def meet(at):
        if at > 0:
            pl.semaphore_wait(met.at[at - 1], len(rounds[at - 1]))
        for peer in rounds[at] if at < len(rounds) else ():
            pl.semaphore_signal(met.at[at], inc=1, device_id=peer, device_id_type=MESH)

    def prepare():
        for load in loads:
            load.wait()
        expert_of = lax.broadcasted_iota(jnp.int32, (EXPERTS * 16, SLOTS), 0) // 16
        match = held_ref[...] == expert_of
        total_rows = jnp.sum(jnp.where(match, share_ref[...].astype(F32), 0.0), axis=1, keepdims=True)
        rows[...] = jnp.broadcast_to(total_rows, rows.shape)
        held = jnp.where(match, 1.0, 0.0).astype(BF16)
        source_of = lax.broadcasted_iota(jnp.int32, (SLOTS, SLOTS * 16), 1) // 16
        spread = jnp.where(lax.broadcasted_iota(jnp.int32, source_of.shape, 0) == source_of, 1.0, 0.0).astype(BF16)
        wide = jnp.dot(held, spread, preferred_element_type=F32)
        same = (lax.broadcasted_iota(jnp.int32, wide.shape, 0) % 16) == (
            lax.broadcasted_iota(jnp.int32, wide.shape, 1) % 16
        )
        sel[...] = jnp.where(same, wide, 0.0).astype(BF16)

    def project(block, p):
        calls.append(block)
        if len(calls) in MEET_AT:
            meet(MEET_AT.index(len(calls)))
        if p is None and not begun:
            prepare()
        columns = pl.ds(pl.multiple_of(block * WIDTH, WIDTH), WIDTH)
        rows = slice(None) if p is None else slice(p * CAP // 2, (p + 1) * CAP // 2)
        term = lax.dot_general(
            weights[:, columns], xs[block, rows, :], (((1,), (1,)), ((), ())), preferred_element_type=F32
        )
        if p is None:
            first = not begun
            begun.append(block)
            if first:
                acc[...] = term
                return
        acc[:, rows] += term

    begun, calls = [], []
    started = ring_gather(
        x_ref.at[0], xs, CAP // 2, (x_ring_send, x_ring_recv, x_mate_send, x_mate_recv), slot, hid, project, EVENLY
    )

    meet(len(rounds))
    gate, up = acc[:UNITS], acc[UNITS:]
    value = (gate / (1.0 + jnp.exp(-gate))) * up
    valid = lax.broadcasted_iota(jnp.int32, value.shape, 1) < counts_ref[slot]
    hidden[hid] = jnp.where(valid, value, 0.0).astype(BF16)

    def exchange(block, p):
        size = UNITS if p is None else UNITS // 2
        base = 0 if p is None else p * size
        terms = jnp.dot(hidden[block, base : base + size, :], cot[...], preferred_element_type=F32)
        for pair in range(size // 24):
            top = 24 * pair
            begin, middle, end = (terms[top + 8 * i : top + 8 * (i + 1)] for i in range(3))
            turned = pltpu.roll(middle, 4, 0)
            owner = block * (UNITS // 12) + (base + top) // 12
            send[owner] = piece_tiles(begin, middle, turned).astype(BF16)
            send[owner + 1] = piece_tiles(end, turned, middle).astype(BF16)
        first = block * (UNITS // 12) + base // 12
        count = size // 12

        @pl.loop(0, count)
        def _(i):
            owner = first + lax.rem(z + i, count)
            @pl.when(owner != slot)
            def _():
                remote(send.at[owner], recv.at[slot], send_sem, recv_sem, (owner, hid)).start()

    started += ring_gather(
        hidden.at[hid], hidden, UNITS // 2, (h_ring_send, h_ring_recv, h_mate_send, h_mate_recv), slot, hid, exchange, EVENLY
    )
    recv[slot] = send[slot]
    for copy in started:
        copy.wait_send()
    wait_bytes(recv.at[pl.ds(0, SLOTS - 1)], recv_sem)

    up, down = lax.rem(z + 1, Z), lax.rem(z + Z - 1, Z)
    group = EXPERTS // GROUPS
    ahead = ((y * Z + up, hid), (y * Z + down, hid))
    hops = []

    def reached(way, step):
        return lax.rem(z + (Z - 1 - step if way == 0 else step + 1), Z)

    def hop(way, step, g):
        block = z if step == 0 else reached(way, step - 1)
        ref = buf.at[block, pl.ds(g * group, group)]
        copy = remote(ref, ref, ring_send.at[way, step, g], ring_recv.at[way, step, g], ahead[way])
        copy.start()
        hops.append(copy)

    def pick(block, to, column_z):
        expert = next_ref[to * Z + column_z]
        chosen = buf[block, 0]
        for e in range(1, EXPERTS):
            chosen = lax.select(expert == e, buf[block, e], chosen)
        return chosen

    def far_copy(way, last):
        if last:
            src, dst = far.at[way, pl.ds(Y, Y // 2)], farthest.at[way]
        else:
            src, dst = picked.at[way], far.at[way]
        return remote(src, dst, far_send.at[way, last], far_recv.at[way, last], ahead[way])

    def to_column(at, blocks, source):
        for d in range(Y):
            to = lax.rem(y + d, Y)
            for way, block in enumerate(blocks):
                chosen = source(way, block, to)
                if d == 0:
                    gathered[y, block] = chosen
                else:
                    stage[d - 1, at, way] = chosen
            if d > 0:
                remote(
                    stage.at[d - 1, at, pl.ds(0, len(blocks))],
                    column.at[d - 1, at, pl.ds(0, len(blocks))],
                    y_send, y_recv.at[d - 1, at], (to * Z + z, hid),
                ).start()

    def to_row(at, blocks):
        for d in range(1, Y):
            ref = column.at[d - 1, at, pl.ds(0, len(blocks))]
            remote(ref, ref, y_send, y_recv.at[d - 1, at], (slot, hid)).wait_recv()
            for way, block in enumerate(blocks):
                gathered[lax.rem(y + Y - d, Y), block] = column[d - 1, at, way]
        if at == Z // 2:
            return
        turn = (at + 1) // 2 * (1 if at % 2 == 0 else -1)
        side = 1 - 2 * lax.rem(z, 2)
        pair = lax.rem(z // 2 + side * turn + Z, Z // 2)
        first = pair * 2
        send_row(first, 2)
        if at == Z // 2 - 2:
            send_row(lax.rem(z - 7 * side + Z, Z), 1)

    def send_row(first, size):
        here, there = pl.ds(first, size), pl.ds(lax.rem(first, Z // 2), size)
        for source in range(Y):
            target = source * CORES + first // (Z // 2)

            @pl.when(target == hid)
            def _():
                land[hid, there] = gathered[source, here]

            @pl.when(target != hid)
            def _():
                remote(gathered.at[source, here], land.at[hid, there], row_send, row_recv, (slot, target)).start()

    def direct(block):
        target = y * CORES + block // (Z // 2)
        for to in range(Y):
            ref = farthest.at[to // (Y // 2), to % (Y // 2)]
            local_one = jnp.logical_and(to == y, target == hid)

            @pl.when(local_one)
            def _():
                land[hid, lax.rem(block, Z // 2)] = ref[...]

            @pl.when(jnp.logical_not(local_one))
            def _():
                remote(
                    ref, land.at[hid, lax.rem(block, Z // 2)], direct_send, direct_recv, (to * Z + z, target)
                ).start()

    def update(part, lines):
        tiles = []
        for t in range(3):
            pieces = recv[:, 16 * t : 16 * (t + 1), :].reshape(SLOTS * 16, 128)
            total = jnp.dot(sel[lines, :], pieces, preferred_element_type=F32) / rows[lines, :]
            total = total.reshape(group, 16, 128)
            tiles += [total[:, :8], total[:, 8:]]
        rest = [tiles[4], pltpu.roll(tiles[4], 4, 1), tiles[5], pltpu.roll(tiles[5], 4, 1)]
        for q in range(4):
            columns = slice(128 * q, 128 * (q + 1))

            @pl.when(slot % 2 == 0)
            def _():
                mean[part, 0:8, columns] = tiles[q]
                mean[part, 8:12, columns] = rest[q][:, :4]

            @pl.when(slot % 2 == 1)
            def _():
                mean[part, 4:12, columns] = tiles[q]
                mean[part, 0:4, columns] = rest[q][:, :4]

        grad[part] = adam(mean[part], master[part], one[part], two[part])[0]
        first, last = grad[part, 0:8, :], grad[part, 4:12, :]

        @pl.when(slot % 2 == 0)
        def _():
            buf[z, part] = piece_tiles(first, pltpu.roll(last, 4, 1), last).astype(BF16)

        @pl.when(slot % 2 == 1)
        def _():
            buf[z, part] = piece_tiles(last, first, pltpu.roll(first, 4, 1)).astype(BF16)

    for g in range(GROUPS):
        update(pl.ds(g * group, group), pl.ds(16 * g * group, 16 * group))
        for way in range(2):
            hop(way, 0, g)
    stores = [pltpu.make_async_copy(mean, mean_ref, mean_sem)]
    stores[0].start()
    here = lambda way, block, to: pick(block, to, z)
    to_column(Z // 2, [z], here)
    behind = [(Z // 2, [z])]
    for step in range(Z // 2):
        ready = [reached(way, step) for way in range(2)]
        if step < NEAR:
            for g in range(GROUPS):
                for way in range(2):
                    ref = buf.at[ready[way], pl.ds(g * group, group)]
                    remote(ref, ref, ring_send.at[way, step, g], ring_recv.at[way, step, g], ahead[way]).wait_recv()
                    if step < NEAR - 1:
                        hop(way, step + 1, g)
            if step == NEAR - 1:
                for way in range(2):
                    one_on, two_on = (lax.rem(z + Z + d * (1 - 2 * way), Z) for d in (1, 2))
                    for to in range(Y):
                        picked[way, to] = pick(ready[way], to, one_on)
                    for to in range(Y // 2):
                        picked[way, Y + to] = pick(ready[way], way * (Y // 2) + to, two_on)
                    hops.append(far_copy(way, 0))
                    hops[-1].start()
            to_column(step, ready, here)
        elif step == NEAR:
            for way in range(2):
                far_copy(way, 0).wait_recv()
                hops.append(far_copy(way, 1))
                hops[-1].start()
            to_column(step, ready, lambda way, block, to: far[way, to])
        else:
            for way in range(2):
                far_copy(way, 1).wait_recv()
            direct(ready[0])
        if step < Z // 2 - 1:
            behind.append((step, ready))
        if step >= LAG - 1:
            to_row(*behind[step + 1 - LAG])
    for item in behind[Z // 2 + 1 - LAG :]:
        to_row(*item)
    far_here = lax.rem(z + Z // 2, Z) // (Z // 2) == core
    near_only = jnp.logical_not(far_here)
    diagonal = jnp.logical_and(far_here, x == y)

    @pl.when(near_only)
    def _():
        wait_bytes(land.at[pl.ds(0, HIDS - 1)], row_recv)

    @pl.when(far_here)
    def _():
        wait_bytes(land.at[pl.ds(0, HIDS - 1), pl.ds(0, Z // 2 - 1)], row_recv)

    @pl.when(diagonal)
    def _():
        wait_bytes(recv.at[pl.ds(0, HIDS - 1)], direct_recv)

    @pl.when(jnp.logical_and(far_here, x != y))
    def _():
        wait_bytes(recv.at[pl.ds(0, HIDS)], direct_recv)

    half = low_half((8, 128))
    for source in range(HIDS):
        columns = []
        for pair in range(Z // 4):
            even, odd = land[source, 2 * pair].astype(F32), land[source, 2 * pair + 1].astype(F32)
            for q in range(4):
                b = slice(32 + 8 * (q // 2), 40 + 8 * (q // 2))
                if q % 2 == 0:
                    middle = jnp.where(half, even[b], pltpu.roll(odd[b], 4, 0))
                else:
                    middle = jnp.where(half, pltpu.roll(even[b], 4, 0), odd[b])
                columns.append((even[8 * q : 8 * q + 8], middle, odd[8 * q : 8 * q + 8]))
        for q in range(4):
            tall = [tile for pair in range(Z // 4) for tile in columns[4 * pair + q]]
            at = WIDTH * source + 128 * q
            placed[:, at : at + 128] = jnp.concatenate(tall, axis=0).astype(BF16)
        stores.append(
            pltpu.make_async_copy(
                placed.at[:, pl.ds(WIDTH * source, WIDTH)],
                out_ref.at[0, :, pl.ds(WIDTH * source, WIDTH)],
                placed_sem.at[source],
            )
        )
        stores[-1].start()
    for copy in hops:
        copy.wait_send()
    for copy in stores:
        copy.wait()
    wait_bytes(send.at[pl.ds(0, SLOTS - 1)], send_sem)
    wait_bytes(recv.at[pl.ds(0, (Y - 1) * (Z - 1))], y_send)
    row_pieces = Y * (Z - 1) - Z // 2

    @pl.when(near_only)
    def _():
        wait_bytes(recv.at[pl.ds(0, row_pieces)], row_send)

    @pl.when(far_here)
    def _():
        wait_bytes(recv.at[pl.ds(0, row_pieces + 1)], row_send)

    @pl.when(diagonal)
    def _():
        wait_bytes(recv.at[pl.ds(0, Y - 1)], direct_send)

    @pl.when(jnp.logical_not(diagonal))
    def _():
        wait_bytes(recv.at[pl.ds(0, Y)], direct_send)


def local(
    inputs, cotangent, w_gate, w_up, counts, place_now, place_next, master, moment_one, moment_two
):
    dma = pltpu.SemaphoreType.DMA
    smem, vmem, hbm = (pl.BlockSpec(memory_space=m) for m in (pltpu.SMEM, pltpu.VMEM, pltpu.HBM))
    state = (EXPERTS, 12, WIDTH)
    update = pl.pallas_call(
        step_kernel,
        out_shape=[jax.ShapeDtypeStruct(state, F32)] + [jax.ShapeDtypeStruct((1, UNITS, FEATURES), BF16)],
        in_specs=[smem, vmem, vmem, smem] + [hbm] * 7,
        out_specs=[hbm] * 2,
        scratch_shapes=[
            pltpu.VMEM((HIDS, CAP, WIDTH), BF16),
            pltpu.VMEM((2 * UNITS, FEATURES), BF16),
            pltpu.VMEM((CAP, WIDTH), BF16),
            pltpu.VMEM((HIDS, UNITS, CAP), BF16),
            pltpu.VMEM((SLOTS,) + PIECE, BF16),
            pltpu.VMEM((SLOTS,) + PIECE, BF16),
            pltpu.VMEM((EXPERTS * 16, SLOTS * 16), BF16),
            pltpu.VMEM((EXPERTS * 16, 128), F32),
            pltpu.VMEM((2 * UNITS, CAP), F32),
            pltpu.VMEM(state, F32), pltpu.VMEM((UNITS, FEATURES), BF16),
            pltpu.VMEM(state, F32), pltpu.VMEM(state, F32), pltpu.VMEM(state, F32), pltpu.VMEM(state, F32),
            pltpu.VMEM((Z, EXPERTS) + PIECE, BF16),
            pltpu.VMEM((Y - 1, Z // 2 + 1, 2) + PIECE, BF16),
            pltpu.VMEM((2, Y + Y // 2) + PIECE, BF16),
            pltpu.VMEM((2, Y + Y // 2) + PIECE, BF16),
            pltpu.VMEM((2, Y // 2) + PIECE, BF16),
            pltpu.VMEM((Y - 1, Z // 2 + 1, 2) + PIECE, BF16),
            pltpu.VMEM((Y, Z) + PIECE, BF16),
            pltpu.VMEM((HIDS, Z // 2) + PIECE, BF16),
            dma((7,)),
            dma((2, 3)), dma((2, 3)), dma((8,)), dma((8,)),
            dma((2, 3)), dma((2, 3)), dma((8,)), dma((8,)),
            dma, dma,
            dma((2, NEAR, GROUPS)), dma((2, NEAR, GROUPS)), dma((2, 2)), dma((2, 2)), dma, dma((Y - 1, Z // 2 + 1)), dma, dma, dma, dma, dma, dma((HIDS,)),
            pltpu.SemaphoreType.REGULAR((3,)),
        ],
        compiler_params=pltpu.CompilerParams(
            collective_id=0, has_side_effects=True, vmem_limit_bytes=60 * 1024 * 1024
        ),
    )
    grad, next_down = update(
        counts, place_now[:, 0][None, :], counts[None, :], place_next[:, 0],
        inputs, cotangent, w_gate, w_up, master, moment_one, moment_two,
    )
    return adam(grad, master, moment_one, moment_two) + (next_down,)


def solution(mesh):
    sharded = P(None, "slot", "hid")
    return jax.shard_map(
        local,
        mesh=mesh,
        in_specs=(
            P("slot", None, "hid"),
            P("slot", None, "hid"),
            P("slot", "hid", None),
            P("slot", "hid", None),
            P(),
            P(),
            P(),
            sharded,
            sharded,
            sharded,
        ),
        out_specs=(sharded, sharded, sharded, P("slot", "hid", None)),
        check_vma=False,
    )
```
